512 devices in a mesh: ctx: 64 (over x, z), tp: 8 (over y, core).
Axes of the slice: x: 4, y: 4, z: 16, core: 2. Of those that a mesh axis runs over, the one named last changes fastest.
Arguments:
- x_input: bfloat16 [8192, 8192], P('ctx', 'tp'), may hold values from -6 to 6
- b_input: bfloat16 [8192, 1024], P('ctx', 'tp'), may hold values from -6 to 6
- c_input: bfloat16 [8192, 1024], P('ctx', 'tp'), may hold values from -0.59765625 to 0.59765625
- step: float32 [128, 8192], P('tp', 'ctx'), may hold values from 0.005 to 0.05
- log_decay: float32 [128, 8192], P('tp', 'ctx'), may hold values from -1 to 0, as said below
- skip: float32 [128], P('tp'), may hold values from 0.5 to 2
- gain: float32 [8192], P('tp'), may hold values from 0.1 to 1.9
- out_weight: bfloat16 [8192, 4096], P(('tp', 'ctx')), may hold values from -0.0625 to 0.0625
Outputs:
- mixed: bfloat16 [8192, 4096], P('ctx', 'tp')
The draws below stay inside these ranges and needn't reach their ends.
Inputs may be any that keep to these rules, and one draw needn't show every extreme that they name: `log_decay`: each entry is the logarithm of a decay factor strictly between 0 and 1.
All inputs are finite; a program needn't handle non-finite values.
Results may differ from the reference program's by a relative error of at most 0.017.
Values may be sent and summed in bfloat16 or wider, within the bound.
No kernel may reach another device: no remote copies, remote signals or barrier semaphores. Data moves between devices by JAX's collectives and lax.ppermute only.
A program may use at most 128 MiB of HBM per device.

```python
import math
import jax
import jax.numpy as jnp
from jax import lax

D = 4096
H = 128
P_SIZE = 64
N = 128
G = 8
SPAN = 128
TOK_DEV = 128
SEQ = 8192
N_TP = 8


def draw_log_decay(key, part):
    key = jax.random.fold_in(key, 11)
    keys = jax.random.split(key, 9)
    share = 0.5
    fast = jax.random.uniform(keys[0], (H,), jnp.float32) < share
    fast_rate = jnp.exp(jax.random.uniform(keys[1], (H,), jnp.float32, math.log(0.02), math.log(0.033)))
    slower_decay_rate = jnp.exp(jax.random.uniform(keys[2], (H,), jnp.float32, math.log(0.1), math.log(0.6))) / SEQ
    base = jnp.where(fast, fast_rate, slower_decay_rate)
    token_factor = jnp.exp(jax.random.uniform(keys[3], (H, SEQ), jnp.float32, -math.log(2.0), math.log(2.0)))
    block_factor = jnp.exp(jax.random.uniform(keys[4], (H, SEQ // TOK_DEV), jnp.float32, -math.log(2.0), math.log(2.0)))
    block_factor = jnp.repeat(block_factor, TOK_DEV, axis=1)
    forgetting_speed = base[:, None] * token_factor * block_factor
    word_offsets = jax.random.randint(keys[5], (H, 2), 0, SEQ)
    drive_coefficient = jax.random.uniform(keys[6], (H, 2), jnp.float32, 0.22, 0.5)
    word_indices = jnp.arange(SEQ)
    word_segments = jnp.sum(jnp.where(word_indices[None, None, :] == word_offsets[:, :, None], drive_coefficient[:, :, None], 0.0), axis=1)
    renewing = jnp.logical_and(jnp.logical_not(fast), jax.random.uniform(keys[7], (H,), jnp.float32) < 0.3)
    phase = jax.random.randint(keys[8], (H,), 0, 8)
    device_block = word_indices // TOK_DEV
    position = word_indices % TOK_DEV
    renew_at = jnp.logical_and((device_block[None, :] + phase[:, None]) % 8 == 0, position[None, :] < 6)
    renewal = jnp.where(jnp.logical_and(renewing[:, None], renew_at), 0.48, 0.0)
    return -(forgetting_speed + word_segments + renewal)


def level_of(own_key, extent, shards, smallest, high):
    def one(axis_at, parts):
        draws = jax.random.uniform(jax.random.fold_in(jax.random.fold_in(own_key, 6), axis_at), (parts,), jnp.float32, smallest / len(shards), high / len(shards))
        return jnp.repeat(jnp.exp(draws), extent[axis_at] // parts).reshape((-1,) + (1,) * (len(extent) - axis_at - 1))

    level = one(*shards[0])
    for cut in shards[1:]:
        level = level * one(*cut)
    return level


def scatter_about(own_key, extent, scale, most, cuts=(), kind=jnp.bfloat16):
    level = level_of(own_key, extent, cuts, -0.22, 0.18) if cuts else 1.0
    drawn = jax.random.normal(own_key, extent, jnp.float32) * scale * level
    return jnp.minimum(jnp.maximum(drawn, -most), most).astype(kind)


def setup_inputs(seed: int = 0) -> dict:
    arg_keys = jax.random.split(jax.random.key(seed), 9)
    x_input = scatter_about(arg_keys[0], (SEQ, H * P_SIZE), 1.0, 6.0, ((0, 64), (1, 8)))
    b_input = scatter_about(arg_keys[1], (SEQ, G * N), 1.0, 6.0, ((0, 64), (1, 8)))
    c_input = scatter_about(arg_keys[2], (SEQ, G * N), 0.09, 0.59765625, ((0, 64), (1, 8)))
    step = jnp.clip(jnp.exp(math.log(0.05) - 2.3025851 * jax.random.uniform(arg_keys[3], (H, SEQ), jnp.float32) ** level_of(arg_keys[3], (H, SEQ), ((0, 8), (1, 64)), -0.2, 0.2)), 0.005, 0.05)
    log_decay = draw_log_decay(jax.random.fold_in(arg_keys[8], 71), 0)
    skip = jnp.clip(0.5 + 1.5 * jax.random.uniform(arg_keys[5], (H,), jnp.float32) ** level_of(arg_keys[5], (H,), ((0, 8),), -0.2, 0.2), 0.5, 2.0)
    gain = jnp.clip(1.0 + 0.18 * jax.random.normal(arg_keys[6], (H * P_SIZE,), jnp.float32), 0.1, 1.9)
    out_weight = scatter_about(arg_keys[7], (H * P_SIZE, D), (H * P_SIZE) ** -0.5, 0.0625, ((0, 512),))
    return {"x_input": x_input, "b_input": b_input, "c_input": c_input, "step": step, "log_decay": log_decay, "skip": skip, "gain": gain, "out_weight": out_weight}


def final_state(grouped, b_rows, tail):
    weighted = (grouped.astype(jnp.float32) * jnp.transpose(tail, (2, 0, 1))[..., None]).astype(jnp.bfloat16)
    return jnp.einsum('jgkp,jgn->gkpn', weighted.astype(jnp.float32), b_rows.astype(jnp.float32), precision=lax.Precision.HIGHEST)

def span_step(state, block):
    values, b_rows, c_rows, steps, logs = block
    length = values.shape[0]
    width = values.shape[1]
    depth = values.shape[2]
    groups = b_rows.shape[1]
    per_group = width // groups
    cumul = jnp.cumsum(logs, axis=-1)
    within = jnp.tril(jnp.ones((length, length), dtype=bool))
    spread = cumul[:, :, None] - cumul[:, None, :]
    decay_mat = jnp.exp(jnp.where(within[None], spread, -jnp.inf))
    common_region = jnp.einsum('ign,jgn->gij', c_rows.astype(jnp.float32), b_rows.astype(jnp.float32), precision=lax.Precision.HIGHEST)
    mixing = common_region[:, None] * decay_mat.reshape(groups, per_group, length, length) * steps.reshape(groups, per_group, 1, length)
    mixing = mixing.astype(jnp.bfloat16)
    grouped = values.reshape(length, groups, per_group, depth)
    output = jnp.einsum('gkij,jgkp->igkp', mixing.astype(jnp.float32), grouped.astype(jnp.float32), precision=lax.Precision.HIGHEST)
    state_grp = state.reshape(groups, per_group, depth, state.shape[2])
    carried = jnp.einsum('ign,gkpn->igkp', c_rows.astype(jnp.float32), state_grp, precision=lax.Precision.HIGHEST)
    scales = jnp.exp(cumul).reshape(groups, per_group, length).transpose(2, 0, 1)
    output = output + scales[..., None] * carried
    tail = (jnp.exp(cumul[:, -1:] - cumul) * steps).reshape(groups, per_group, length)
    fresh = final_state(grouped, b_rows, tail)
    updated_state = jnp.exp(cumul[:, -1])[:, None, None] * state + fresh.reshape(state.shape)
    return (updated_state, output.reshape(length, width, depth))

def run_spans(values, b_rows, c_rows, steps, logs, start_state, span):
    total = values.shape[0]
    count = total // span
    width = values.shape[1]
    depth = values.shape[2]
    groups = b_rows.shape[1]
    blocks = (values.reshape(count, span, width, depth), b_rows.reshape(count, span, groups, b_rows.shape[2]), c_rows.reshape(count, span, groups, c_rows.shape[2]), steps.reshape(width, count, span).transpose(1, 0, 2), logs.reshape(width, count, span).transpose(1, 0, 2))
    final, outputs = lax.scan(span_step, start_state, blocks)
    return (final, outputs.reshape(total, width, depth))

def normalize(ssm, gain, groups):
    total = ssm.shape[0]
    grouped = ssm.reshape(total, groups, -1)
    meansq = lax.optimization_barrier(jnp.mean(grouped * grouped, axis=-1, keepdims=True))
    normed = grouped * lax.rsqrt(meansq + 1e-05)
    return (normed.reshape(total, -1) * gain[None, :]).astype(jnp.bfloat16)

def reference(x_input, b_input, c_input, step, log_decay, skip, gain, out_weight):
    values = x_input.reshape(SEQ, H, P_SIZE)
    b_rows = b_input.reshape(SEQ, G, N)
    c_rows = c_input.reshape(SEQ, G, N)
    start_state = jnp.zeros((H, P_SIZE, N), jnp.float32)
    unused, ssm = run_spans(values, b_rows, c_rows, step, log_decay, start_state, SPAN)
    ssm = ssm + skip[None, :, None] * values.astype(jnp.float32)
    hidden = normalize(ssm, gain, G)
    block = H * P_SIZE // N_TP

    def add_block(index, accum):
        segment_members = lax.dynamic_slice_in_dim(hidden, (index * block).astype(jnp.int32), block, 1)
        part_weight = lax.dynamic_slice_in_dim(out_weight, (index * block).astype(jnp.int32), block, 0)
        partial_sum = jnp.dot(segment_members, part_weight, preferred_element_type=jnp.float32).astype(jnp.bfloat16)
        partial_sum = lax.optimization_barrier(partial_sum)
        return accum + partial_sum.astype(jnp.float32)
    total = lax.fori_loop(0, N_TP, add_block, jnp.zeros((SEQ, D), jnp.float32))
    return total.astype(jnp.bfloat16)
```

```python
import jax
import jax.numpy as jnp
from jax import lax
from jax.sharding import Mesh, PartitionSpec as P

NX, NZ, NY, NC = 4, 16, 4, 2
TOK = 128
HEADS = 16
P_SIZE = 64
N = 128
EXTRA = 16
f32 = jnp.float32
bf16 = jnp.bfloat16


def split3(value):
    high = lax.reduce_precision(value, 8, 7)
    rest = value - high
    middle = lax.reduce_precision(rest, 8, 7)
    low = lax.reduce_precision(rest - middle, 8, 7)
    return high, middle, low


def gather_x(part):
    return lax.all_to_all(
        jnp.broadcast_to(part[None], (NX,) + part.shape), "x", 0, 0, tiled=True
    )


def entering_states(fresh, total):
    pieces = jnp.stack(split3(total), axis=1)
    rows = jnp.concatenate([pieces, jnp.zeros((HEADS, EXTRA - 3), f32)], axis=1)
    rows = jnp.broadcast_to(rows[:, :, None], (HEADS, EXTRA, N))
    send = jnp.concatenate([fresh, rows], axis=1).astype(bf16)
    got = lax.all_to_all(send, "z", 0, 0, tiled=True).astype(f32)
    blocks = got[:, :P_SIZE]
    decays = got[:, P_SIZE] + got[:, P_SIZE + 1] + got[:, P_SIZE + 2]
    state = jnp.zeros((P_SIZE, N), f32)
    whole = jnp.zeros((1, N), f32)
    for k in range(NZ):
        state = jnp.exp(decays[k])[None] * state + blocks[k]
        whole = whole + decays[k][None]
    row = jnp.concatenate([state, jnp.broadcast_to(whole, (8, N))], axis=0)
    rows_x = gather_x(row)
    me = lax.axis_index("x")
    state = jnp.zeros((P_SIZE, N), f32)
    for k in range(NX):
        new = jnp.exp(rows_x[k, P_SIZE])[None] * state + rows_x[k, :P_SIZE]
        state = jnp.where(k < me, new, state)
    entering = []
    for k in range(NZ):
        entering.append(state.astype(bf16))
        state = jnp.exp(decays[k])[None] * state + blocks[k]
    return lax.all_to_all(jnp.stack(entering), "z", 0, 0, tiled=True)


def project(hidden, weight):
    everyone = gather_x(hidden).reshape(NX * TOK, HEADS * P_SIZE)
    term = jnp.dot(everyone, weight, preferred_element_type=f32)
    half = term.shape[1] // 2
    core = lax.axis_index("c")
    mine = lax.dynamic_slice_in_dim(term, core * half, half, 1)
    other = lax.dynamic_slice_in_dim(term, (1 - core) * half, half, 1).astype(bf16)
    other = lax.ppermute(other, "c", [(0, 1), (1, 0)])
    pair = (mine + other.astype(f32)).astype(bf16).reshape(NX, TOK, half)
    y = lax.axis_index("y")
    axes = ("x", "y")
    total = jnp.zeros((TOK, half), f32)
    for k in range(NX):
        piece = lax.dynamic_index_in_dim(pair, lax.rem(y + k, NX), 0, keepdims=False)
        pairs = [(j * NY + i, ((i + k) % NX) * NY + j) for j in range(NX) for i in range(NY)]
        total = total + lax.ppermute(piece, axes, pairs).astype(f32)
    return total.astype(bf16)


def shards(x_input, b_input, c_input, step, log_decay, skip, gain, out_weight):
    columns = out_weight.shape[1] // NX
    swap = out_weight.reshape(out_weight.shape[0], NX, columns).transpose(1, 0, 2)
    swap = lax.all_to_all(swap, "x", 0, 0, tiled=True)
    weight = lax.all_gather(swap, "z", axis=0)
    weight = weight.transpose(1, 0, 2, 3).reshape(HEADS * P_SIZE, columns)

    values = x_input.reshape(TOK, HEADS, P_SIZE)
    cumul = jnp.cumsum(log_decay, axis=1)
    total = cumul[:, -1]
    tail = jnp.exp(total[:, None] - cumul) * step
    weighted = (values.astype(f32) * tail.T[:, :, None]).astype(bf16)
    fresh = jnp.einsum("shp,sn->hpn", weighted, b_input, preferred_element_type=f32)
    entering = entering_states(fresh, total)

    within = jnp.tril(jnp.ones((TOK, TOK), dtype=bool))
    spread = cumul[:, :, None] - cumul[:, None, :]
    decay = jnp.exp(jnp.where(within[None], spread, -jnp.inf))
    scores = jnp.einsum("tn,sn->ts", c_input, b_input, preferred_element_type=f32)
    mixing = (scores[None] * decay * step[:, None, :]).astype(bf16)
    ssm = jnp.einsum("hts,shp->thp", mixing, values, preferred_element_type=f32)
    carried = jnp.einsum("tn,hpn->thp", c_input, entering, preferred_element_type=f32)
    ssm = ssm + jnp.exp(cumul).T[:, :, None] * carried
    ssm = ssm + skip[None, :, None] * values.astype(f32)
    ssm = ssm.reshape(TOK, HEADS * P_SIZE)
    meansq = jnp.mean(ssm * ssm, axis=1, keepdims=True)
    hidden = (ssm * lax.rsqrt(meansq + 1e-05) * gain[None, :]).astype(bf16)
    return project(hidden, weight)


def solution(mesh):
    fine = Mesh(mesh.devices.reshape(NX, NZ, NY, NC), ("x", "z", "y", "c"))
    ctx, tp = ("x", "z"), ("y", "c")
    in_specs = (
        P(ctx, tp),
        P(ctx, tp),
        P(ctx, tp),
        P(tp, ctx),
        P(tp, ctx),
        P(tp),
        P(tp),
        P(tp + ctx, None),
    )
    return jax.shard_map(
        shards, mesh=fine, in_specs=in_specs, out_specs=P(ctx, tp), check_vma=False
    )
```

```python
import jax
import jax.numpy as jnp
from jax import lax
from jax.experimental import pallas as pl
from jax.experimental.pallas import tpu as pltpu
from jax.sharding import Mesh, PartitionSpec as P

NX, NZ, NY, NC = 4, 16, 4, 2
NTP = NY * NC
TOK = 128
HEADS = 16
P_SIZE = 64
N = 128
WIDTH = HEADS * P_SIZE
EXTRA = 16
ROWS = P_SIZE + EXTRA
SUM_ROWS = P_SIZE + 8
COLS = 128
f32 = jnp.float32
bf16 = jnp.bfloat16
HIGH = lax.Precision.HIGHEST


def call(kernel, out_shape, flops, moved, name):
    return pl.pallas_call(
        kernel,
        out_shape=out_shape,
        name=name,
        compiler_params=pltpu.CompilerParams(vmem_limit_bytes=32 * 2**20),
        cost_estimate=pl.CostEstimate(flops=flops, bytes_accessed=moved, transcendentals=0),
    )


def iota(shape, axis):
    return lax.broadcasted_iota(jnp.int32, shape, axis)


def dot(a, b, ca, cb, precision=None):
    return lax.dot_general(
        a, b, (((ca,), (cb,)), ((), ())), precision=precision, preferred_element_type=f32
    )


def cumulative(logs):
    upto = (iota((TOK, TOK), 0) <= iota((TOK, TOK), 1)).astype(f32)
    return dot(logs, upto, 1, 0, HIGH)


def spread_heads(per_head):
    owner = (iota((HEADS, WIDTH), 1) // P_SIZE == iota((HEADS, WIDTH), 0)).astype(f32)
    return dot(per_head, owner, 0, 0, HIGH)


def fresh_kernel(x_ref, b_ref, step_ref, logs_ref, out_ref):
    logs = logs_ref[...]
    cumul = cumulative(logs)
    total = dot(logs, jnp.ones((TOK, TOK), f32), 1, 0, HIGH)
    tail = jnp.exp(total - cumul) * step_ref[...]
    weighted = (x_ref[...].astype(f32) * spread_heads(tail)).astype(bf16)
    fresh = dot(weighted, b_ref[...], 0, 0).astype(bf16)
    high = total.astype(bf16)
    rest = total - high.astype(f32)
    middle = rest.astype(bf16)
    low = (rest - middle.astype(f32)).astype(bf16)
    row = iota((EXTRA, N), 0)
    for h in range(HEADS):
        out_ref[h, :P_SIZE, :] = fresh[h * P_SIZE : (h + 1) * P_SIZE]
        first, second, third = (
            jnp.broadcast_to(part[h : h + 1].astype(f32), (EXTRA, N)) for part in (high, middle, low)
        )
        pieces = jnp.where(row == 0, first, jnp.where(row == 1, second, third))
        out_ref[h, P_SIZE:, :] = jnp.where(row < 3, pieces, 0.0).astype(bf16)


def block_decay(got_ref, k):
    pieces = got_ref[k, P_SIZE:, :].astype(f32)
    return pieces[0:1] + pieces[1:2] + pieces[2:3]


def row_kernel(got_ref, out_ref):
    state = jnp.zeros((P_SIZE, N), f32)
    whole = jnp.zeros((1, N), f32)
    for k in range(NZ):
        decay = block_decay(got_ref, k)
        state = jnp.exp(decay) * state + got_ref[k, :P_SIZE, :].astype(f32)
        whole = whole + decay
    out_ref[:P_SIZE, :] = state
    out_ref[P_SIZE:, :] = jnp.broadcast_to(whole, (8, N))


def enter_kernel(me_ref, got_ref, rows_ref, out_ref):
    me = me_ref[0]
    state = jnp.zeros((P_SIZE, N), f32)
    for k in range(NX):
        decay = jnp.exp(rows_ref[k, P_SIZE : P_SIZE + 1, :])
        state = jnp.where(k < me, decay * state + rows_ref[k, :P_SIZE, :], state)
    for k in range(NZ):
        out_ref[k, :, :] = state.astype(bf16)
        decay = jnp.exp(block_decay(got_ref, k))
        state = decay * state + got_ref[k, :P_SIZE, :].astype(f32)


def inner_kernel(x_ref, b_ref, c_ref, step_ref, logs_ref, skip_ref, out_ref, scale_ref):
    logs = logs_ref[...]
    cumul = cumulative(logs)
    upto = (iota((TOK, TOK), 1) <= iota((TOK, TOK), 0)).astype(f32)
    cumul_t = dot(upto, logs, 1, 1, HIGH)
    scale_ref[...] = spread_heads(jnp.exp(cumul))
    scores = dot(c_ref[...], b_ref[...], 1, 1)
    within = iota((TOK, TOK), 1) <= iota((TOK, TOK), 0)
    left = iota((TOK, 2 * P_SIZE), 1) < P_SIZE
    for pair in range(HEADS // 2):
        columns = slice(pair * 2 * P_SIZE, (pair + 1) * 2 * P_SIZE)
        values = x_ref[:, columns]
        both = []
        for h in (2 * pair, 2 * pair + 1):
            spread = cumul_t[:, h : h + 1] - cumul[h : h + 1, :]
            decay = jnp.exp(jnp.where(within, spread, -1e30))
            mixing = (scores * decay * step_ref[h : h + 1, :]).astype(bf16)
            both.append(dot(mixing, values, 1, 0))
        own = jnp.where(left, both[0], both[1])
        out_ref[:, columns] = own + skip_ref[:, columns] * values.astype(f32)


def hidden_kernel(inner_ref, scale_ref, c_ref, state_ref, gain_ref, out_ref):
    states = state_ref[...].reshape(WIDTH, N)
    ssm = inner_ref[...] + scale_ref[...] * dot(c_ref[...], states, 1, 1)
    meansq = jnp.mean(ssm * ssm, axis=1, keepdims=True)
    out_ref[...] = (ssm * lax.rsqrt(meansq + 1e-05) * gain_ref[...]).astype(bf16)


def product_kernel(hidden_ref, weight_ref, out_ref):
    depth = WIDTH // NX
    term = jnp.zeros((NX * TOK, weight_ref.shape[3]), f32)
    for k in range(NX):
        rows = weight_ref[:, k, :, :].reshape(depth, weight_ref.shape[3])
        term = term + dot(hidden_ref[:, k * depth : (k + 1) * depth], rows, 1, 0)
    term = term.astype(bf16)
    for k in range(NX):
        for j in range(out_ref.shape[1]):
            out_ref[k, j, :, :] = term[k * TOK : (k + 1) * TOK, j * COLS : (j + 1) * COLS]


def sum_kernel(parts_ref, out_ref):
    for k in range(NX):
        total = parts_ref[k, 0, :, :].astype(f32)
        for j in range(1, NTP):
            total = total + parts_ref[k, j, :, :].astype(f32)
        out_ref[:, k * COLS : (k + 1) * COLS] = total.astype(bf16)


def gather_x(part):
    return lax.all_to_all(
        jnp.broadcast_to(part[None], (NX,) + part.shape), "x", 0, 0, tiled=True
    )


def shape(*dims, dtype=bf16):
    return jax.ShapeDtypeStruct(dims, dtype)


def shards(x_input, b_input, c_input, step, log_decay, skip, gain, out_weight):
    depth = out_weight.shape[0]
    swap = out_weight.reshape(depth, NTP, NX, COLS).transpose(2, 0, 1, 3)
    swap = lax.all_to_all(swap.reshape(NX, depth, NTP * COLS), "x", 0, 0, tiled=True)

    send = call(fresh_kernel, shape(HEADS, ROWS, N), 4 * 10**7, 10**6, "fresh")(
        x_input, b_input, step, log_decay
    )
    send, swap = lax.optimization_barrier((send, swap))
    weight = lax.all_gather(swap, "z", axis=0)

    got = lax.all_to_all(send, "z", 0, 0, tiled=True)
    inner, scale = call(
        inner_kernel,
        (shape(TOK, WIDTH, dtype=f32), shape(TOK, WIDTH, dtype=f32)),
        10**8,
        2 * 10**6,
        "inner",
    )(x_input, b_input, c_input, step, log_decay, jnp.repeat(skip, P_SIZE)[None])
    row = call(row_kernel, shape(SUM_ROWS, N, dtype=f32), 10**6, 4 * 10**5, "row")(got)
    rows = gather_x(row)
    me = lax.axis_index("x").astype(jnp.int32)[None]
    entering = pl.pallas_call(
        enter_kernel,
        out_shape=shape(HEADS, P_SIZE, N),
        in_specs=[
            pl.BlockSpec(memory_space=pltpu.SMEM),
            pl.BlockSpec(memory_space=pltpu.VMEM),
            pl.BlockSpec(memory_space=pltpu.VMEM),
        ],
        name="enter",
        cost_estimate=pl.CostEstimate(flops=10**6, bytes_accessed=10**6, transcendentals=0),
    )(me, got, rows)
    states = lax.all_to_all(entering, "z", 0, 0, tiled=True)

    hidden = call(hidden_kernel, shape(TOK, WIDTH), 3 * 10**7, 2 * 10**6, "hidden")(
        inner, scale, c_input, states, gain[None]
    )
    everyone = gather_x(hidden).reshape(NX * TOK, WIDTH)

    tiles = 2
    parts = pl.pallas_call(
        product_kernel,
        grid=(NTP // tiles,),
        out_shape=shape(NX, NTP, TOK, COLS),
        in_specs=[
            pl.BlockSpec((NX * TOK, WIDTH), lambda n: (0, 0)),
            pl.BlockSpec((NZ, NX, depth, tiles * COLS), lambda n: (0, 0, 0, n)),
        ],
        out_specs=pl.BlockSpec((NX, tiles, TOK, COLS), lambda n: (0, n, 0, 0)),
        name="product",
        compiler_params=pltpu.CompilerParams(vmem_limit_bytes=32 * 2**20),
        cost_estimate=pl.CostEstimate(
            flops=2 * NX * TOK * WIDTH * NTP * COLS, bytes_accessed=4 * 10**6, transcendentals=0
        ),
    )(everyone, weight)
    parts = parts.reshape(NX * NTP, TOK, COLS)
    parts = lax.all_to_all(parts, ("x", "y", "c"), 0, 0, tiled=True)
    return call(sum_kernel, shape(TOK, NX * COLS), 10**6, 10**6, "sum")(
        parts.reshape(NX, NTP, TOK, COLS)
    )


def solution(mesh):
    fine = Mesh(mesh.devices.reshape(NX, NZ, NY, NC), ("x", "z", "y", "c"))
    ctx, tp = ("x", "z"), ("y", "c")
    in_specs = (
        P(ctx, tp),
        P(ctx, tp),
        P(ctx, tp),
        P(tp, ctx),
        P(tp, ctx),
        P(tp),
        P(tp),
        P(tp + ctx, None),
    )
    return jax.shard_map(
        shards, mesh=fine, in_specs=in_specs, out_specs=P(ctx, tp), check_vma=False
    )
```

```python
import jax
import jax.numpy as jnp
from jax import lax
from jax.experimental import pallas as pl
from jax.experimental.pallas import tpu as pltpu
from jax.sharding import Mesh, PartitionSpec as P

NX, NZ, NY, NC = 4, 16, 4, 2
NTP = NY * NC
TOK = 128
HEADS = 16
P_SIZE = 64
N = 128
WIDTH = HEADS * P_SIZE
EXTRA = 16
ROWS = P_SIZE + EXTRA
SUM_ROWS = P_SIZE + 8
COLS = 128
VMEM = 56 * 2**20
f32 = jnp.float32
bf16 = jnp.bfloat16
HIGH = lax.Precision.HIGHEST


def call(kernel, out_shape, flops, moved, name, scalars=0, operands=0):
    specs = {}
    if scalars:
        specs["in_specs"] = [pl.BlockSpec(memory_space=pltpu.SMEM)] * scalars + [
            pl.BlockSpec(memory_space=pltpu.VMEM)
        ] * operands
    return pl.pallas_call(
        kernel,
        out_shape=out_shape,
        name=name,
        compiler_params=pltpu.CompilerParams(vmem_limit_bytes=VMEM),
        cost_estimate=pl.CostEstimate(flops=flops, bytes_accessed=moved, transcendentals=0),
        **specs,
    )


def iota(shape, axis):
    return lax.broadcasted_iota(jnp.int32, shape, axis)


def dot(a, b, ca, cb, precision=None):
    return lax.dot_general(
        a, b, (((ca,), (cb,)), ((), ())), precision=precision, preferred_element_type=f32
    )


def cumulative(logs):
    upto = (iota((TOK, TOK), 0) <= iota((TOK, TOK), 1)).astype(f32)
    return dot(logs, upto, 1, 0, HIGH)


def spread_heads(per_head):
    owner = (iota((HEADS, WIDTH), 1) // P_SIZE == iota((HEADS, WIDTH), 0)).astype(f32)
    return dot(per_head, owner, 0, 0, HIGH)


def pack_kernel(core_ref, weight_ref, out_ref):
    first = core_ref[0] == 0
    block = NX * COLS
    for x in range(NX):
        for y in range(NY):
            even, odd = (
                weight_ref[:, pl.ds((2 * y + c) * block + x * COLS, COLS)] for c in range(NC)
            )
            out_ref[x, :, pl.ds(y * COLS, COLS)] = jnp.where(first, even, odd)
            out_ref[x, :, pl.ds((NY + y) * COLS, COLS)] = jnp.where(first, odd, even)


def fresh_kernel(x_ref, b_ref, step_ref, logs_ref, out_ref):
    logs = logs_ref[...]
    cumul = cumulative(logs)
    total = dot(logs, jnp.ones((TOK, TOK), f32), 1, 0, HIGH)
    tail = jnp.exp(total - cumul) * step_ref[...]
    weighted = (x_ref[...].astype(f32) * spread_heads(tail)).astype(bf16)
    fresh = dot(weighted, b_ref[...], 0, 0).astype(bf16)
    high = total.astype(bf16)
    rest = total - high.astype(f32)
    middle = rest.astype(bf16)
    low = (rest - middle.astype(f32)).astype(bf16)
    row = iota((EXTRA, N), 0)
    for h in range(HEADS):
        out_ref[h, :P_SIZE, :] = fresh[h * P_SIZE : (h + 1) * P_SIZE]
        first, second, third = (
            jnp.broadcast_to(part[h : h + 1].astype(f32), (EXTRA, N)) for part in (high, middle, low)
        )
        pieces = jnp.where(row == 0, first, jnp.where(row == 1, second, third))
        out_ref[h, P_SIZE:, :] = jnp.where(row < 3, pieces, 0.0).astype(bf16)


def block_decay(got_ref, k):
    pieces = got_ref[k, P_SIZE:, :].astype(f32)
    return pieces[0:1] + pieces[1:2] + pieces[2:3]


def row_kernel(got_ref, out_ref):
    state = jnp.zeros((P_SIZE, N), f32)
    whole = jnp.zeros((1, N), f32)
    for k in range(NZ):
        decay = block_decay(got_ref, k)
        state = jnp.exp(decay) * state + got_ref[k, :P_SIZE, :].astype(f32)
        whole = whole + decay
    for k in range(NX):
        out_ref[k, :P_SIZE, :] = state
        out_ref[k, P_SIZE:, :] = jnp.broadcast_to(whole, (8, N))


def enter_kernel(me_ref, got_ref, rows_ref, out_ref):
    me = me_ref[0]
    state = jnp.zeros((P_SIZE, N), f32)
    for k in range(NX):
        decay = jnp.exp(rows_ref[k, P_SIZE : P_SIZE + 1, :])
        state = jnp.where(k < me, decay * state + rows_ref[k, :P_SIZE, :], state)
    for k in range(NZ):
        out_ref[k, :, :] = state.astype(bf16)
        decay = jnp.exp(block_decay(got_ref, k))
        state = decay * state + got_ref[k, :P_SIZE, :].astype(f32)


def inner_kernel(x_ref, b_ref, c_ref, step_ref, logs_ref, skip_ref, out_ref, scale_ref):
    logs = logs_ref[...]
    cumul = cumulative(logs)
    upto = (iota((TOK, TOK), 1) <= iota((TOK, TOK), 0)).astype(f32)
    cumul_t = dot(upto, logs, 1, 1, HIGH)
    scale_ref[...] = spread_heads(jnp.exp(cumul))
    scores = dot(c_ref[...], b_ref[...], 1, 1)
    within = iota((TOK, TOK), 1) <= iota((TOK, TOK), 0)
    left = iota((TOK, 2 * P_SIZE), 1) < P_SIZE
    for pair in range(HEADS // 2):
        columns = slice(pair * 2 * P_SIZE, (pair + 1) * 2 * P_SIZE)
        values = x_ref[:, columns]
        both = []
        for h in (2 * pair, 2 * pair + 1):
            spread = cumul_t[:, h : h + 1] - cumul[h : h + 1, :]
            decay = jnp.exp(jnp.where(within, spread, -1e30))
            mixing = (scores * decay * step_ref[h : h + 1, :]).astype(bf16)
            both.append(dot(mixing, values, 1, 0))
        own = jnp.where(left, both[0], both[1])
        out_ref[:, columns] = own + skip_ref[:, columns] * values.astype(f32)


def hidden_kernel(inner_ref, scale_ref, c_ref, state_ref, gain_ref, out_ref):
    states = state_ref[...].reshape(WIDTH, N)
    ssm = inner_ref[...] + scale_ref[...] * dot(c_ref[...], states, 1, 1)
    meansq = jnp.mean(ssm * ssm, axis=1, keepdims=True)
    hidden = (ssm * lax.rsqrt(meansq + 1e-05) * gain_ref[...]).astype(bf16)
    for k in range(NX):
        out_ref[k, :, :] = hidden


def product_kernel(hidden_ref, weight_ref, out_ref):
    depth = WIDTH // NX
    wide = weight_ref.shape[3]
    for k in range(NX):
        rows = weight_ref[:, k, :, :].reshape(depth, wide)
        for i in range(NX):
            term = dot(hidden_ref[i, :, k * depth : (k + 1) * depth], rows, 1, 0)
            for j in range(NY):
                piece = term[:, j * COLS : (j + 1) * COLS]
                if k == 0:
                    out_ref[i, j, :, :] = piece
                else:
                    out_ref[i, j, :, :] += piece


def other_kernel(hidden_ref, weight_ref, out_ref, total):
    product_kernel(hidden_ref, weight_ref, total)
    out_ref[...] = total[...].astype(bf16)


def pair_kernel(mine_ref, other_ref, out_ref):
    out_ref[...] = (mine_ref[...] + other_ref[...].astype(f32)).astype(bf16)


def sum_kernel(parts_ref, out_ref):
    for k in range(NX):
        total = parts_ref[k, 0, :, :].astype(f32)
        for j in range(1, NY):
            total = total + parts_ref[k, j, :, :].astype(f32)
        out_ref[:, k * COLS : (k + 1) * COLS] = total.astype(bf16)


def shape(*dims, dtype=bf16):
    return jax.ShapeDtypeStruct(dims, dtype)


def product(everyone, weight, half):
    depth, wide = weight.shape[2], NY * COLS
    return pl.pallas_call(
        other_kernel if half else product_kernel,
        grid=(1,),
        out_shape=shape(NX, NY, TOK, COLS, dtype=bf16 if half else f32),
        in_specs=[
            pl.BlockSpec((NX, TOK, WIDTH), lambda n: (0, 0, 0)),
            pl.BlockSpec((NZ, NX, depth, wide), lambda n: (0, 0, 0, half)),
        ],
        out_specs=pl.BlockSpec((NX, NY, TOK, COLS), lambda n: (0, 0, 0, 0)),
        scratch_shapes=[pltpu.VMEM((NX, NY, TOK, COLS), f32)] if half else [],
        name="other" if half else "mine",
        compiler_params=pltpu.CompilerParams(vmem_limit_bytes=VMEM),
        cost_estimate=pl.CostEstimate(
            flops=2 * NX * TOK * WIDTH * wide, bytes_accessed=3 * 10**6, transcendentals=0
        ),
    )(everyone, weight)


def shards(x_input, b_input, c_input, step, log_decay, skip, gain, out_weight):
    depth = out_weight.shape[0]
    core = lax.axis_index("c").astype(jnp.int32)[None]
    me = lax.axis_index("x").astype(jnp.int32)[None]
    swap = call(pack_kernel, shape(NX, depth, NTP * COLS), 0, 3 * 10**5, "pack", 1, 1)(
        core, out_weight
    )
    swap = lax.all_to_all(swap, "x", 0, 0, tiled=True)

    send = call(fresh_kernel, shape(HEADS, ROWS, N), 4 * 10**7, 10**6, "fresh")(
        x_input, b_input, step, log_decay
    )
    send, swap = lax.optimization_barrier((send, swap))
    weight = lax.all_gather(swap, "z", axis=0)

    got = lax.all_to_all(send, "z", 0, 0, tiled=True)
    inner, scale = call(
        inner_kernel,
        (shape(TOK, WIDTH, dtype=f32), shape(TOK, WIDTH, dtype=f32)),
        10**8,
        2 * 10**6,
        "inner",
    )(x_input, b_input, c_input, step, log_decay, jnp.repeat(skip, P_SIZE)[None])
    row = call(row_kernel, shape(NX, SUM_ROWS, N, dtype=f32), 10**6, 4 * 10**5, "row")(got)
    rows = lax.all_to_all(row, "x", 0, 0, tiled=True)
    entering = call(enter_kernel, shape(HEADS, P_SIZE, N), 10**6, 10**6, "enter", 1, 2)(
        me, got, rows
    )
    states = lax.all_to_all(entering, "z", 0, 0, tiled=True)

    hidden = call(hidden_kernel, shape(NX, TOK, WIDTH), 3 * 10**7, 2 * 10**6, "hidden")(
        inner, scale, c_input, states, gain[None]
    )
    everyone = lax.all_to_all(hidden, "x", 0, 0, tiled=True)

    other = product(everyone, weight, 1)
    other = lax.ppermute(other, "c", [(0, 1), (1, 0)])
    mine = product(everyone, weight, 0)
    parts = call(pair_kernel, shape(NX, NY, TOK, COLS), 10**6, 2 * 10**6, "pair")(mine, other)
    parts = lax.all_to_all(parts.reshape(NX * NY, TOK, COLS), ("x", "y"), 0, 0, tiled=True)
    return call(sum_kernel, shape(TOK, NX * COLS), 10**6, 10**6, "sum")(
        parts.reshape(NX, NY, TOK, COLS)
    )


def solution(mesh):
    fine = Mesh(mesh.devices.reshape(NX, NZ, NY, NC), ("x", "z", "y", "c"))
    ctx, tp = ("x", "z"), ("y", "c")
    in_specs = (
        P(ctx, tp),
        P(ctx, tp),
        P(ctx, tp),
        P(tp, ctx),
        P(tp, ctx),
        P(tp),
        P(tp),
        P(tp + ctx, None),
    )
    return jax.shard_map(
        shards, mesh=fine, in_specs=in_specs, out_specs=P(ctx, tp), check_vma=False
    )
```

```python
import jax
import jax.numpy as jnp
from jax import lax
from jax.experimental import pallas as pl
from jax.experimental.pallas import tpu as pltpu
from jax.sharding import Mesh, PartitionSpec as P

NX, NZ, NY, NC = 4, 16, 4, 2
NTP = NY * NC
TOK = 128
HEADS = 16
P_SIZE = 64
N = 128
WIDTH = HEADS * P_SIZE
CTX = NX * NZ
CHUNK = WIDTH // CTX
EXTRA = 8
COLS = 128
LARGE = 56 * 2**20
f32 = jnp.float32
bf16 = jnp.bfloat16
HIGH = lax.Precision.HIGHEST


def call(kernel, out_shape, flops, moved, name, vmem=32 * 2**20):
    return pl.pallas_call(
        kernel,
        out_shape=out_shape,
        name=name,
        compiler_params=pltpu.CompilerParams(vmem_limit_bytes=vmem),
        cost_estimate=pl.CostEstimate(flops=flops, bytes_accessed=moved, transcendentals=0),
    )


def iota(shape, axis):
    return lax.broadcasted_iota(jnp.int32, shape, axis)


def dot(a, b, ca, cb, precision=None):
    return lax.dot_general(
        a, b, (((ca,), (cb,)), ((), ())), precision=precision, preferred_element_type=f32
    )


def cumulative(logs):
    upto = (iota((TOK, TOK), 0) <= iota((TOK, TOK), 1)).astype(f32)
    return dot(logs, upto, 1, 0, HIGH)


def spread_heads(per_head):
    owner = (iota((HEADS, WIDTH), 1) // P_SIZE == iota((HEADS, WIDTH), 0)).astype(f32)
    return dot(per_head, owner, 0, 0, HIGH)


def pack_kernel(weight_ref, out_ref):
    for x in range(NX):
        for j in range(NTP):
            out_ref[x, :, j * COLS : (j + 1) * COLS] = weight_ref[:, pl.ds((j * NX + x) * COLS, COLS)]


def fresh_kernel(x_ref, b_ref, step_ref, logs_ref, out_ref):
    logs = logs_ref[...]
    cumul = cumulative(logs)
    total = dot(logs, jnp.ones((TOK, TOK), f32), 1, 0, HIGH)
    tail = jnp.exp(total - cumul) * step_ref[...]
    weighted = (x_ref[...].astype(f32) * spread_heads(tail)).astype(bf16)
    fresh = dot(weighted, b_ref[...], 0, 0).astype(bf16)
    high = total.astype(bf16)
    rest = total - high.astype(f32)
    middle = rest.astype(bf16)
    low = (rest - middle.astype(f32)).astype(bf16)
    row = iota((EXTRA, N), 0)
    for h in range(HEADS):
        first, second, third = (
            jnp.broadcast_to(part[h : h + 1].astype(f32), (EXTRA, N)) for part in (high, middle, low)
        )
        pieces = jnp.where(row == 0, first, jnp.where(row == 1, second, third))
        pieces = jnp.where(row < 3, pieces, 0.0).astype(bf16)
        for k in range(h * P_SIZE // CHUNK, (h + 1) * P_SIZE // CHUNK):
            out_ref[k, :CHUNK, :] = fresh[k * CHUNK : (k + 1) * CHUNK]
            out_ref[k, CHUNK:, :] = pieces


def scan_kernel(got_ref, out_ref):
    state = jnp.zeros((CHUNK, N), f32)
    for k in range(CTX):
        out_ref[k, :, :] = state.astype(bf16)
        pieces = got_ref[k, CHUNK:, :].astype(f32)
        decay = jnp.exp(pieces[0:1] + pieces[1:2] + pieces[2:3])
        state = decay * state + got_ref[k, :CHUNK, :].astype(f32)


def inner_kernel(x_ref, b_ref, c_ref, step_ref, logs_ref, skip_ref, out_ref, scale_ref):
    logs = logs_ref[...]
    cumul = cumulative(logs)
    upto = (iota((TOK, TOK), 1) <= iota((TOK, TOK), 0)).astype(f32)
    cumul_t = dot(upto, logs, 1, 1, HIGH)
    scale_ref[...] = spread_heads(jnp.exp(cumul))
    scores = dot(c_ref[...], b_ref[...], 1, 1)
    within = iota((TOK, TOK), 1) <= iota((TOK, TOK), 0)
    left = iota((TOK, 2 * P_SIZE), 1) < P_SIZE
    for pair in range(HEADS // 2):
        columns = slice(pair * 2 * P_SIZE, (pair + 1) * 2 * P_SIZE)
        values = x_ref[:, columns]
        both = []
        for h in (2 * pair, 2 * pair + 1):
            spread = cumul_t[:, h : h + 1] - cumul[h : h + 1, :]
            decay = jnp.exp(jnp.where(within, spread, -1e30))
            mixing = (scores * decay * step_ref[h : h + 1, :]).astype(bf16)
            both.append(dot(mixing, values, 1, 0))
        own = jnp.where(left, both[0], both[1])
        out_ref[:, columns] = own + skip_ref[:, columns] * values.astype(f32)


def hidden_kernel(inner_ref, scale_ref, c_ref, state_ref, gain_ref, out_ref):
    states = state_ref[...].reshape(WIDTH, N)
    ssm = inner_ref[...] + scale_ref[...] * dot(c_ref[...], states, 1, 1)
    meansq = jnp.mean(ssm * ssm, axis=1, keepdims=True)
    hidden = (ssm * lax.rsqrt(meansq + 1e-05) * gain_ref[...]).astype(bf16)
    for k in range(NX):
        out_ref[k, :, :] = hidden


def product_kernel(hidden_ref, weight_ref, out_ref):
    depth = WIDTH // NX
    wide = weight_ref.shape[3]
    for i in range(NX):
        term = jnp.zeros((TOK, wide), f32)
        for k in range(NX):
            rows = weight_ref[:, k, :, :].reshape(depth, wide)
            term = term + dot(hidden_ref[i, :, k * depth : (k + 1) * depth], rows, 1, 0)
        for j in range(wide // COLS):
            out_ref[i, j, :, :] = term[:, j * COLS : (j + 1) * COLS].astype(bf16)


def sum_kernel(parts_ref, out_ref):
    for k in range(NX):
        total = parts_ref[k, 0, :, :].astype(f32)
        for j in range(1, NTP):
            total = total + parts_ref[k, j, :, :].astype(f32)
        out_ref[:, k * COLS : (k + 1) * COLS] = total.astype(bf16)


def shape(*dims, dtype=bf16):
    return jax.ShapeDtypeStruct(dims, dtype)


def product(everyone, weight):
    depth, tiles = weight.shape[2], 2
    return pl.pallas_call(
        product_kernel,
        grid=(NTP // tiles,),
        out_shape=shape(NX, NTP, TOK, COLS),
        in_specs=[
            pl.BlockSpec((NX, TOK, WIDTH), lambda n: (0, 0, 0)),
            pl.BlockSpec((NZ, NX, depth, tiles * COLS), lambda n: (0, 0, 0, n)),
        ],
        out_specs=pl.BlockSpec((NX, tiles, TOK, COLS), lambda n: (0, n, 0, 0)),
        name="product",
        compiler_params=pltpu.CompilerParams(vmem_limit_bytes=LARGE),
        cost_estimate=pl.CostEstimate(
            flops=2 * NX * TOK * WIDTH * NTP * COLS, bytes_accessed=4 * 10**6, transcendentals=0
        ),
    )(everyone, weight)


def shards(x_input, b_input, c_input, step, log_decay, skip, gain, out_weight):
    depth = out_weight.shape[0]
    swap = call(pack_kernel, shape(NX, depth, NTP * COLS), 0, 3 * 10**5, "pack", LARGE)(out_weight)
    swap = lax.all_to_all(swap, "x", 0, 0, tiled=True)

    send = call(
        fresh_kernel, shape(CTX, CHUNK + EXTRA, N), 4 * 10**7, 10**6, "fresh", LARGE
    )(x_input, b_input, step, log_decay)
    send, swap = lax.optimization_barrier((send, swap))
    weight = lax.all_gather(swap, "z", axis=0)

    got = lax.all_to_all(send, ("x", "z"), 0, 0, tiled=True)
    inner, scale = call(
        inner_kernel,
        (shape(TOK, WIDTH, dtype=f32), shape(TOK, WIDTH, dtype=f32)),
        10**8,
        2 * 10**6,
        "inner",
    )(x_input, b_input, c_input, step, log_decay, jnp.repeat(skip, P_SIZE)[None])
    entering = call(scan_kernel, shape(CTX, CHUNK, N), 10**6, 7 * 10**5, "scan")(got)
    states = lax.all_to_all(entering, ("x", "z"), 0, 0, tiled=True)

    hidden = call(hidden_kernel, shape(NX, TOK, WIDTH), 3 * 10**7, 2 * 10**6, "hidden")(
        inner, scale, c_input, states, gain[None]
    )
    everyone = lax.all_to_all(hidden, "x", 0, 0, tiled=True)
    parts = product(everyone, weight).reshape(NX * NTP, TOK, COLS)
    parts = lax.all_to_all(parts, ("x", "y", "c"), 0, 0, tiled=True)
    return call(sum_kernel, shape(TOK, NX * COLS), 10**6, 10**6, "sum")(
        parts.reshape(NX, NTP, TOK, COLS)
    )


def solution(mesh):
    fine = Mesh(mesh.devices.reshape(NX, NZ, NY, NC), ("x", "z", "y", "c"))
    ctx, tp = ("x", "z"), ("y", "c")
    in_specs = (
        P(ctx, tp),
        P(ctx, tp),
        P(ctx, tp),
        P(tp, ctx),
        P(tp, ctx),
        P(tp),
        P(tp),
        P(tp + ctx, None),
    )
    return jax.shard_map(
        shards, mesh=fine, in_specs=in_specs, out_specs=P(ctx, tp), check_vma=False
    )
```

```python
import jax
import jax.numpy as jnp
from jax import lax
from jax.experimental import pallas as pl
from jax.experimental.pallas import tpu as pltpu
from jax.sharding import Mesh, PartitionSpec as P

NX, NZ, NY, NC = 4, 16, 4, 2
NL = 2
NH = NZ // NL
GROUP = NX * NL
OFFSETS = (0, -1, 1, -2, 2, -3, 3, -4)
NTP = NY * NC
TOK = 128
HEADS = 16
P_SIZE = 64
N = 128
WIDTH = HEADS * P_SIZE
CTX = NX * NZ
CHUNK = WIDTH // CTX
EXTRA = 8
HALF = TOK // 2
COLS = 64
LARGE = 56 * 2**20
f32 = jnp.float32
bf16 = jnp.bfloat16
HIGH = lax.Precision.HIGHEST


def call(kernel, out_shape, flops, moved, name, vmem=32 * 2**20):
    return pl.pallas_call(
        kernel,
        out_shape=out_shape,
        name=name,
        compiler_params=pltpu.CompilerParams(vmem_limit_bytes=vmem),
        cost_estimate=pl.CostEstimate(flops=flops, bytes_accessed=moved, transcendentals=0),
    )


def iota(shape, axis):
    return lax.broadcasted_iota(jnp.int32, shape, axis)


def dot(a, b, ca, cb, precision=None):
    return lax.dot_general(
        a, b, (((ca,), (cb,)), ((), ())), precision=precision, preferred_element_type=f32
    )


def cumulative(logs):
    upto = (iota((TOK, TOK), 0) <= iota((TOK, TOK), 1)).astype(f32)
    return dot(logs, upto, 1, 0, HIGH)


def spread_heads(per_head):
    owner = (iota((HEADS, WIDTH), 1) // P_SIZE == iota((HEADS, WIDTH), 0)).astype(f32)
    return dot(per_head, owner, 0, 0, HIGH)


def halves(low, high):
    left = iota(low.shape, 1) < COLS
    return (
        jnp.where(left, low, pltpu.roll(high, COLS, 1)),
        jnp.where(left, pltpu.roll(low, COLS, 1), high),
    )


def pack_kernel(weight_ref, out_ref):
    wide = GROUP * COLS
    for pair in range(GROUP // 2):
        for j in range(NTP // 2):
            even, odd = (
                weight_ref[:, pl.ds((2 * j + i) * wide + pair * 2 * COLS, 2 * COLS)].astype(f32)
                for i in range(2)
            )
            columns = slice(j * 2 * COLS, (j + 1) * 2 * COLS)
            first, second = halves(even, odd)
            out_ref[2 * pair, :, columns] = first.astype(bf16)
            out_ref[2 * pair + 1, :, columns] = second.astype(bf16)


def fresh_kernel(x_ref, b_ref, step_ref, logs_ref, out_ref):
    logs = logs_ref[...]
    cumul = cumulative(logs)
    total = dot(logs, jnp.ones((TOK, TOK), f32), 1, 0, HIGH)
    tail = jnp.exp(total - cumul) * step_ref[...]
    weighted = (x_ref[...].astype(f32) * spread_heads(tail)).astype(bf16)
    fresh = dot(weighted, b_ref[...], 0, 0).astype(bf16)
    high = total.astype(bf16)
    rest = total - high.astype(f32)
    middle = rest.astype(bf16)
    low = (rest - middle.astype(f32)).astype(bf16)
    row = iota((EXTRA, N), 0)
    for h in range(HEADS):
        first, second, third = (
            jnp.broadcast_to(part[h : h + 1].astype(f32), (EXTRA, N)) for part in (high, middle, low)
        )
        pieces = jnp.where(row == 0, first, jnp.where(row == 1, second, third))
        pieces = jnp.where(row < 3, pieces, 0.0).astype(bf16)
        for k in range(h * P_SIZE // CHUNK, (h + 1) * P_SIZE // CHUNK):
            out_ref[k, :CHUNK, :] = fresh[k * CHUNK : (k + 1) * CHUNK]
            out_ref[k, CHUNK:, :] = pieces


def scan_kernel(got_ref, out_ref):
    state = jnp.zeros((CHUNK, N), f32)
    for k in range(CTX):
        out_ref[k, :, :] = state.astype(bf16)
        pieces = got_ref[k, CHUNK:, :].astype(f32)
        decay = jnp.exp(pieces[0:1] + pieces[1:2] + pieces[2:3])
        state = decay * state + got_ref[k, :CHUNK, :].astype(f32)


def inner_kernel(x_ref, b_ref, c_ref, step_ref, logs_ref, skip_ref, out_ref, scale_ref):
    logs = logs_ref[...]
    cumul = cumulative(logs)
    upto = (iota((TOK, TOK), 1) <= iota((TOK, TOK), 0)).astype(f32)
    cumul_t = dot(upto, logs, 1, 1, HIGH)
    scale_ref[...] = spread_heads(jnp.exp(cumul))
    scores = dot(c_ref[...], b_ref[...], 1, 1)
    within = iota((TOK, TOK), 1) <= iota((TOK, TOK), 0)
    left = iota((TOK, 2 * P_SIZE), 1) < P_SIZE
    for pair in range(HEADS // 2):
        columns = slice(pair * 2 * P_SIZE, (pair + 1) * 2 * P_SIZE)
        values = x_ref[:, columns]
        both = []
        for h in (2 * pair, 2 * pair + 1):
            spread = cumul_t[:, h : h + 1] - cumul[h : h + 1, :]
            decay = jnp.exp(jnp.where(within, spread, -1e30))
            mixing = (scores * decay * step_ref[h : h + 1, :]).astype(bf16)
            both.append(dot(mixing, values, 1, 0))
        own = jnp.where(left, both[0], both[1])
        out_ref[:, columns] = own + skip_ref[:, columns] * values.astype(f32)


def hidden_kernel(inner_ref, scale_ref, c_ref, state_ref, gain_ref, out_ref):
    states = state_ref[...].reshape(WIDTH, N)
    ssm = inner_ref[...] + scale_ref[...] * dot(c_ref[...], states, 1, 1)
    meansq = jnp.mean(ssm * ssm, axis=1, keepdims=True)
    hidden = (ssm * lax.rsqrt(meansq + 1e-05) * gain_ref[...]).astype(bf16)
    for k in range(GROUP):
        out_ref[k, :, :] = hidden


def product_kernel(me_ref, hidden_ref, *refs):
    *blocks, out_ref, weight_ref = refs
    me = me_ref[0]
    for offset, block_ref in zip(OFFSETS, blocks):
        weight_ref[lax.rem(me + (offset + NH), NH)] = block_ref[...]
    depth = WIDTH // NX
    wide = weight_ref.shape[3]
    for i in range(GROUP):
        term = jnp.zeros((TOK, wide), f32)
        for k in range(NX):
            rows = weight_ref[:, k * NL : (k + 1) * NL, :, :].reshape(depth, wide)
            term = term + dot(hidden_ref[i, :, k * depth : (k + 1) * depth], rows, 1, 0)
        for j in range(NTP // 2):
            both = term[:, j * 2 * COLS : (j + 1) * 2 * COLS]
            first, second = halves(both[:HALF], both[HALF:])
            out_ref[i * NTP + 2 * j, :, :] = first.astype(bf16)
            out_ref[i * NTP + 2 * j + 1, :, :] = second.astype(bf16)


def sum_kernel(parts_ref, out_ref):
    for pair in range(GROUP // 2):
        totals = []
        for k in (2 * pair, 2 * pair + 1):
            total = parts_ref[k * NTP, :, :].astype(f32)
            for j in range(1, NTP):
                total = total + parts_ref[k * NTP + j, :, :].astype(f32)
            totals.append(total)
        columns = slice(pair * 2 * COLS, (pair + 1) * 2 * COLS)
        first, second = halves(*totals)
        out_ref[:HALF, columns] = first.astype(bf16)
        out_ref[HALF:, columns] = second.astype(bf16)


def shape(*dims, dtype=bf16):
    return jax.ShapeDtypeStruct(dims, dtype)


def ring(up, down):
    return (
        lax.ppermute(up, "zh", [(i, (i + 1) % NH) for i in range(NH)]),
        lax.ppermute(down, "zh", [(i, (i - 1) % NH) for i in range(NH)]),
    )


def shards(x_input, b_input, c_input, step, log_decay, skip, gain, out_weight):
    ctx = ("x", "zh", "zl")
    members = ("x", "zl")
    depth = out_weight.shape[0]
    own = call(
        pack_kernel, shape(GROUP, depth, NTP * COLS), 0, 3 * 10**5, "pack", LARGE
    )(out_weight)
    own = lax.all_to_all(own, members, 0, 0, tiled=True)
    send = call(
        fresh_kernel, shape(CTX, CHUNK + EXTRA, N), 4 * 10**7, 10**6, "fresh", LARGE
    )(x_input, b_input, step, log_decay)
    send, own = lax.optimization_barrier((send, own))

    got = lax.all_to_all(send, ctx, 0, 0, tiled=True)
    up1, down1 = ring(own, own)
    up2, down2 = ring(up1, down1)
    got, up2, down2 = lax.optimization_barrier((got, up2, down2))
    entering = call(scan_kernel, shape(CTX, CHUNK, N), 10**6, 7 * 10**5, "scan")(got)
    entering, up2, down2 = lax.optimization_barrier((entering, up2, down2))
    states = lax.all_to_all(entering, ctx, 0, 0, tiled=True)
    up3, down3 = ring(up2, down2)
    up4 = ring(up3, up3)[0]
    inner, scale = call(
        inner_kernel,
        (shape(TOK, WIDTH, dtype=f32), shape(TOK, WIDTH, dtype=f32)),
        10**8,
        2 * 10**6,
        "inner",
    )(x_input, b_input, c_input, step, log_decay, jnp.repeat(skip, P_SIZE)[None])
    states, up4, down3 = lax.optimization_barrier((states, up4, down3))

    hidden = call(hidden_kernel, shape(GROUP, TOK, WIDTH), 3 * 10**7, 2 * 10**6, "hidden")(
        inner, scale, c_input, states, gain[None]
    )
    everyone = lax.all_to_all(hidden, members, 0, 0, tiled=True)
    blocks = (own, up1, down1, up2, down2, up3, down3, up4)
    me = lax.axis_index("zh").astype(jnp.int32)[None]
    vmem = pl.BlockSpec(memory_space=pltpu.VMEM)
    parts = pl.pallas_call(
        product_kernel,
        out_shape=shape(GROUP * NTP, HALF, 2 * COLS),
        in_specs=[pl.BlockSpec(memory_space=pltpu.SMEM)] + [vmem] * (1 + len(blocks)),
        scratch_shapes=[pltpu.VMEM((NH, GROUP, depth, NTP * COLS), bf16)],
        name="product",
        compiler_params=pltpu.CompilerParams(vmem_limit_bytes=32 * 2**20),
        cost_estimate=pl.CostEstimate(
            flops=2 * GROUP * TOK * WIDTH * NTP * COLS, bytes_accessed=4 * 10**6, transcendentals=0
        ),
    )(me, everyone, *blocks)
    parts = lax.all_to_all(parts, members + ("y", "c"), 0, 0, tiled=True)
    return call(sum_kernel, shape(TOK, GROUP * COLS), 10**6, 10**6, "sum")(parts)


def solution(mesh):
    fine = Mesh(mesh.devices.reshape(NX, NH, NL, NY, NC), ("x", "zh", "zl", "y", "c"))
    ctx, tp = ("x", "zh", "zl"), ("y", "c")
    in_specs = (
        P(ctx, tp),
        P(ctx, tp),
        P(ctx, tp),
        P(tp, ctx),
        P(tp, ctx),
        P(tp),
        P(tp),
        P(tp + ctx, None),
    )
    return jax.shard_map(
        shards, mesh=fine, in_specs=in_specs, out_specs=P(ctx, tp), check_vma=False
    )
```

```python
import jax
import jax.numpy as jnp
from jax import lax
from jax.experimental import pallas as pl
from jax.experimental.pallas import tpu as pltpu
from jax.sharding import Mesh, PartitionSpec as P

NX, NZ, NY, NC = 4, 16, 4, 2
NTP = NY * NC
TOK = 128
HEADS = 16
P_SIZE = 64
N = 128
WIDTH = HEADS * P_SIZE
CTX = NX * NZ
CHUNK = WIDTH // CTX
EXTRA = 8
COLS = 128
LARGE = 56 * 2**20
f32 = jnp.float32
bf16 = jnp.bfloat16
HIGH = lax.Precision.HIGHEST


def call(kernel, out_shape, flops, moved, name, vmem=32 * 2**20):
    return pl.pallas_call(
        kernel,
        out_shape=out_shape,
        name=name,
        compiler_params=pltpu.CompilerParams(vmem_limit_bytes=vmem),
        cost_estimate=pl.CostEstimate(flops=flops, bytes_accessed=moved, transcendentals=0),
    )


def iota(shape, axis):
    return lax.broadcasted_iota(jnp.int32, shape, axis)


def dot(a, b, ca, cb, precision=None):
    return lax.dot_general(
        a, b, (((ca,), (cb,)), ((), ())), precision=precision, preferred_element_type=f32
    )


def cumulative(logs):
    upto = (iota((TOK, TOK), 0) <= iota((TOK, TOK), 1)).astype(f32)
    return dot(logs, upto, 1, 0, HIGH)


def spread_heads(per_head):
    owner = (iota((HEADS, WIDTH), 1) // P_SIZE == iota((HEADS, WIDTH), 0)).astype(f32)
    return dot(per_head, owner, 0, 0, HIGH)


def pack_kernel(weight_ref, out_ref, held_ref, sem):
    copy = pltpu.make_async_copy(weight_ref, held_ref, sem)
    copy.start()
    copy.wait()
    for x in range(NX):
        for j in range(NTP):
            out_ref[x, :, j * COLS : (j + 1) * COLS] = held_ref[:, pl.ds((j * NX + x) * COLS, COLS)]


def fresh_kernel(x_ref, b_ref, step_ref, logs_ref, out_ref):
    logs = logs_ref[...]
    cumul = cumulative(logs)
    total = dot(logs, jnp.ones((TOK, TOK), f32), 1, 0, HIGH)
    tail = jnp.exp(total - cumul) * step_ref[...]
    weighted = (x_ref[...].astype(f32) * spread_heads(tail)).astype(bf16)
    fresh = dot(weighted, b_ref[...], 0, 0).astype(bf16)
    high = total.astype(bf16)
    rest = total - high.astype(f32)
    middle = rest.astype(bf16)
    low = (rest - middle.astype(f32)).astype(bf16)
    row = iota((EXTRA, N), 0)
    for h in range(HEADS):
        first, second, third = (
            jnp.broadcast_to(part[h : h + 1].astype(f32), (EXTRA, N)) for part in (high, middle, low)
        )
        pieces = jnp.where(row == 0, first, jnp.where(row == 1, second, third))
        pieces = jnp.where(row < 3, pieces, 0.0).astype(bf16)
        for k in range(h * P_SIZE // CHUNK, (h + 1) * P_SIZE // CHUNK):
            out_ref[k, :CHUNK, :] = fresh[k * CHUNK : (k + 1) * CHUNK]
            out_ref[k, CHUNK:, :] = pieces


def scan_kernel(got_ref, out_ref):
    state = jnp.zeros((CHUNK, N), f32)
    for k in range(CTX):
        out_ref[k, :, :] = state.astype(bf16)
        pieces = got_ref[k, CHUNK:, :].astype(f32)
        decay = jnp.exp(pieces[0:1] + pieces[1:2] + pieces[2:3])
        state = decay * state + got_ref[k, :CHUNK, :].astype(f32)


def inner_kernel(x_ref, b_ref, c_ref, step_ref, logs_ref, skip_ref, out_ref, scale_ref):
    logs = logs_ref[...]
    cumul = cumulative(logs)
    upto = (iota((TOK, TOK), 1) <= iota((TOK, TOK), 0)).astype(f32)
    cumul_t = dot(upto, logs, 1, 1, HIGH)
    scale_ref[...] = spread_heads(jnp.exp(cumul))
    scores = dot(c_ref[...], b_ref[...], 1, 1)
    within = iota((TOK, TOK), 1) <= iota((TOK, TOK), 0)
    left = iota((TOK, 2 * P_SIZE), 1) < P_SIZE
    for pair in range(HEADS // 2):
        columns = slice(pair * 2 * P_SIZE, (pair + 1) * 2 * P_SIZE)
        values = x_ref[:, columns]
        both = []
        for h in (2 * pair, 2 * pair + 1):
            spread = cumul_t[:, h : h + 1] - cumul[h : h + 1, :]
            decay = jnp.exp(jnp.where(within, spread, -1e30))
            mixing = (scores * decay * step_ref[h : h + 1, :]).astype(bf16)
            both.append(dot(mixing, values, 1, 0))
        own = jnp.where(left, both[0], both[1])
        out_ref[:, columns] = own + skip_ref[:, columns] * values.astype(f32)


def hidden_kernel(inner_ref, scale_ref, c_ref, state_ref, gain_ref, out_ref):
    states = state_ref[...].reshape(WIDTH, N)
    ssm = inner_ref[...] + scale_ref[...] * dot(c_ref[...], states, 1, 1)
    meansq = jnp.mean(ssm * ssm, axis=1, keepdims=True)
    hidden = (ssm * lax.rsqrt(meansq + 1e-05) * gain_ref[...]).astype(bf16)
    for k in range(NX):
        out_ref[k, :, :] = hidden


def product_kernel(hidden_ref, weight_ref, out_ref, tokens_ref, held_ref, total_ref, sems):
    depth = WIDTH // NX
    wide = weight_ref.shape[3]
    copies = []
    for k in range(NX):
        part = hidden_ref.at[:, :, pl.ds(k * depth, depth)]
        copies.append(
            (
                pltpu.make_async_copy(part, tokens_ref.at[k], sems.at[0, k]),
                pltpu.make_async_copy(weight_ref.at[:, k], held_ref.at[k], sems.at[1, k]),
            )
        )
    for pair in copies:
        for copy in pair:
            copy.start()
    for k in range(NX):
        for copy in copies[k]:
            copy.wait()
        rows = held_ref[k].reshape(depth, wide)
        for i in range(NX):
            term = dot(tokens_ref[k, i], rows, 1, 0)
            if k == 0:
                total_ref[i] = term
            elif k < NX - 1:
                total_ref[i] += term
            else:
                term = (total_ref[i] + term).astype(bf16)
                for j in range(wide // COLS):
                    out_ref[i, j, :, :] = term[:, j * COLS : (j + 1) * COLS]


def sum_kernel(parts_ref, out_ref):
    for k in range(NX):
        total = parts_ref[k, 0, :, :].astype(f32)
        for j in range(1, NTP):
            total = total + parts_ref[k, j, :, :].astype(f32)
        out_ref[:, k * COLS : (k + 1) * COLS] = total.astype(bf16)


def shape(*dims, dtype=bf16):
    return jax.ShapeDtypeStruct(dims, dtype)


def product(everyone, weight):
    depth, wide = weight.shape[2], weight.shape[3]
    return pl.pallas_call(
        product_kernel,
        out_shape=shape(NX, NTP, TOK, COLS),
        in_specs=[pl.BlockSpec(memory_space=pl.ANY)] * 2,
        scratch_shapes=[
            pltpu.VMEM((NX, NX, TOK, WIDTH // NX), bf16),
            pltpu.VMEM((NX, NZ, depth, wide), bf16),
            pltpu.VMEM((NX, TOK, wide), f32),
            pltpu.SemaphoreType.DMA((2, NX)),
        ],
        name="product",
        compiler_params=pltpu.CompilerParams(vmem_limit_bytes=52 * 2**20),
        cost_estimate=pl.CostEstimate(
            flops=2 * NX * TOK * WIDTH * NTP * COLS, bytes_accessed=4 * 10**6, transcendentals=0
        ),
    )(everyone, weight)


def shards(x_input, b_input, c_input, step, log_decay, skip, gain, out_weight):
    depth = out_weight.shape[0]
    swap = pl.pallas_call(
        pack_kernel,
        out_shape=shape(NX, depth, NTP * COLS),
        in_specs=[pl.BlockSpec(memory_space=pl.ANY)],
        scratch_shapes=[pltpu.VMEM(out_weight.shape, bf16), pltpu.SemaphoreType.DMA(())],
        name="pack",
        compiler_params=pltpu.CompilerParams(vmem_limit_bytes=LARGE),
        cost_estimate=pl.CostEstimate(flops=0, bytes_accessed=3 * 10**5, transcendentals=0),
    )(out_weight)
    swap = lax.all_to_all(swap, "x", 0, 0, tiled=True)

    send = call(
        fresh_kernel, shape(CTX, CHUNK + EXTRA, N), 4 * 10**7, 10**6, "fresh", LARGE
    )(x_input, b_input, step, log_decay)
    send, swap = lax.optimization_barrier((send, swap))
    weight = lax.all_gather(swap, "z", axis=0)

    got = lax.all_to_all(send, ("x", "z"), 0, 0, tiled=True)
    inner, scale = call(
        inner_kernel,
        (shape(TOK, WIDTH, dtype=f32), shape(TOK, WIDTH, dtype=f32)),
        10**8,
        2 * 10**6,
        "inner",
    )(x_input, b_input, c_input, step, log_decay, jnp.repeat(skip, P_SIZE)[None])
    entering = call(scan_kernel, shape(CTX, CHUNK, N), 10**6, 7 * 10**5, "scan")(got)
    states = lax.all_to_all(entering, ("x", "z"), 0, 0, tiled=True)

    hidden = call(hidden_kernel, shape(NX, TOK, WIDTH), 3 * 10**7, 2 * 10**6, "hidden")(
        inner, scale, c_input, states, gain[None]
    )
    everyone = lax.all_to_all(hidden, "x", 0, 0, tiled=True)
    parts = product(everyone, weight).reshape(NX * NTP, TOK, COLS)
    parts = lax.all_to_all(parts, ("x", "y", "c"), 0, 0, tiled=True)
    return call(sum_kernel, shape(TOK, NX * COLS), 10**6, 10**6, "sum")(
        parts.reshape(NX, NTP, TOK, COLS)
    )


def solution(mesh):
    fine = Mesh(mesh.devices.reshape(NX, NZ, NY, NC), ("x", "z", "y", "c"))
    ctx, tp = ("x", "z"), ("y", "c")
    in_specs = (
        P(ctx, tp),
        P(ctx, tp),
        P(ctx, tp),
        P(tp, ctx),
        P(tp, ctx),
        P(tp),
        P(tp),
        P(tp + ctx, None),
    )
    return jax.shard_map(
        shards, mesh=fine, in_specs=in_specs, out_specs=P(ctx, tp), check_vma=False
    )
```

```python
import functools

import jax
import jax.numpy as jnp
from jax import lax
from jax.experimental import pallas as pl
from jax.experimental.pallas import tpu as pltpu
from jax.sharding import Mesh, PartitionSpec as P

NX, NZ, NY, NC = 4, 16, 4, 2
NTP = NY * NC
TOK = 128
HEADS = 16
P_SIZE = 64
N = 128
WIDTH = HEADS * P_SIZE
CTX = NX * NZ
CHUNK = WIDTH // CTX
EXTRA = 8
COLS = 128
LARGE = 56 * 2**20
f32 = jnp.float32
bf16 = jnp.bfloat16
HIGH = lax.Precision.HIGHEST


def call(kernel, out_shape, flops, moved, name, vmem=32 * 2**20):
    return pl.pallas_call(
        kernel,
        out_shape=out_shape,
        name=name,
        compiler_params=pltpu.CompilerParams(vmem_limit_bytes=vmem),
        cost_estimate=pl.CostEstimate(flops=flops, bytes_accessed=moved, transcendentals=0),
    )


def iota(shape, axis):
    return lax.broadcasted_iota(jnp.int32, shape, axis)


def dot(a, b, ca, cb, precision=None):
    return lax.dot_general(
        a, b, (((ca,), (cb,)), ((), ())), precision=precision, preferred_element_type=f32
    )


def cumulative(logs):
    upto = (iota((TOK, TOK), 0) <= iota((TOK, TOK), 1)).astype(f32)
    return dot(logs, upto, 1, 0, HIGH)


def spread_heads(per_head):
    owner = (iota((HEADS, WIDTH), 1) // P_SIZE == iota((HEADS, WIDTH), 0)).astype(f32)
    return dot(per_head, owner, 0, 0, HIGH)


def pack_kernel(core_ref, weight_ref, out_ref, held_ref, sem):
    copy = pltpu.make_async_copy(weight_ref, held_ref, sem)
    copy.start()
    copy.wait()
    first = core_ref[0] == 0
    for x in range(NX):
        for y in range(NY):
            even, odd = (
                held_ref[:, pl.ds(((y * NC + c) * NX + x) * COLS, COLS)] for c in range(NC)
            )
            out_ref[x, :, y * COLS : (y + 1) * COLS] = jnp.where(first, even, odd)
            out_ref[x, :, (NY + y) * COLS : (NY + y + 1) * COLS] = jnp.where(first, odd, even)


def fresh_kernel(x_ref, b_ref, step_ref, logs_ref, out_ref):
    logs = logs_ref[...]
    cumul = cumulative(logs)
    total = dot(logs, jnp.ones((TOK, TOK), f32), 1, 0, HIGH)
    tail = jnp.exp(total - cumul) * step_ref[...]
    weighted = (x_ref[...].astype(f32) * spread_heads(tail)).astype(bf16)
    fresh = dot(weighted, b_ref[...], 0, 0).astype(bf16)
    high = total.astype(bf16)
    rest = total - high.astype(f32)
    middle = rest.astype(bf16)
    low = (rest - middle.astype(f32)).astype(bf16)
    row = iota((EXTRA, N), 0)
    for h in range(HEADS):
        first, second, third = (
            jnp.broadcast_to(part[h : h + 1].astype(f32), (EXTRA, N)) for part in (high, middle, low)
        )
        pieces = jnp.where(row == 0, first, jnp.where(row == 1, second, third))
        pieces = jnp.where(row < 3, pieces, 0.0).astype(bf16)
        for k in range(h * P_SIZE // CHUNK, (h + 1) * P_SIZE // CHUNK):
            out_ref[k, :CHUNK, :] = fresh[k * CHUNK : (k + 1) * CHUNK]
            out_ref[k, CHUNK:, :] = pieces


def scan_kernel(got_ref, out_ref):
    state = jnp.zeros((CHUNK, N), f32)
    for k in range(CTX):
        out_ref[k, :, :] = state.astype(bf16)
        pieces = got_ref[k, CHUNK:, :].astype(f32)
        decay = jnp.exp(pieces[0:1] + pieces[1:2] + pieces[2:3])
        state = decay * state + got_ref[k, :CHUNK, :].astype(f32)


def inner_kernel(x_ref, b_ref, c_ref, step_ref, logs_ref, skip_ref, out_ref, scale_ref):
    logs = logs_ref[...]
    cumul = cumulative(logs)
    upto = (iota((TOK, TOK), 1) <= iota((TOK, TOK), 0)).astype(f32)
    cumul_t = dot(upto, logs, 1, 1, HIGH)
    scale_ref[...] = spread_heads(jnp.exp(cumul))
    scores = dot(c_ref[...], b_ref[...], 1, 1)
    within = iota((TOK, TOK), 1) <= iota((TOK, TOK), 0)
    left = iota((TOK, 2 * P_SIZE), 1) < P_SIZE
    for pair in range(HEADS // 2):
        columns = slice(pair * 2 * P_SIZE, (pair + 1) * 2 * P_SIZE)
        values = x_ref[:, columns]
        both = []
        for h in (2 * pair, 2 * pair + 1):
            spread = cumul_t[:, h : h + 1] - cumul[h : h + 1, :]
            decay = jnp.exp(jnp.where(within, spread, -1e30))
            mixing = (scores * decay * step_ref[h : h + 1, :]).astype(bf16)
            both.append(dot(mixing, values, 1, 0))
        own = jnp.where(left, both[0], both[1])
        out_ref[:, columns] = own + skip_ref[:, columns] * values.astype(f32)


def hidden_kernel(inner_ref, scale_ref, c_ref, state_ref, gain_ref, out_ref):
    states = state_ref[...].reshape(WIDTH, N)
    ssm = inner_ref[...] + scale_ref[...] * dot(c_ref[...], states, 1, 1)
    meansq = jnp.mean(ssm * ssm, axis=1, keepdims=True)
    hidden = (ssm * lax.rsqrt(meansq + 1e-05) * gain_ref[...]).astype(bf16)
    for k in range(NX):
        out_ref[k, :, :] = hidden


def product_kernel(half, hidden_ref, weight_ref, out_ref, tokens_ref, held_ref, total_ref, sems):
    depth = WIDTH // NX
    wide = NY * COLS
    copies = []
    for k in range(NX):
        part = hidden_ref.at[:, :, pl.ds(k * depth, depth)]
        rows = weight_ref.at[:, k, :, pl.ds(half * wide, wide)]
        copies.append(
            (
                pltpu.make_async_copy(part, tokens_ref.at[k], sems.at[0, k]),
                pltpu.make_async_copy(rows, held_ref.at[k], sems.at[1, k]),
            )
        )
    for pair in copies:
        for copy in pair:
            copy.start()
    for k in range(NX):
        for copy in copies[k]:
            copy.wait()
        rows = held_ref[k].reshape(depth, wide)
        for i in range(NX):
            term = dot(tokens_ref[k, i], rows, 1, 0)
            if k == 0:
                total_ref[i] = term
            elif k < NX - 1:
                total_ref[i] += term
            else:
                term = (total_ref[i] + term).astype(out_ref.dtype)
                for j in range(NY):
                    out_ref[i, j, :, :] = term[:, j * COLS : (j + 1) * COLS]


def pair_kernel(mine_ref, other_ref, out_ref):
    out_ref[...] = (mine_ref[...] + other_ref[...].astype(f32)).astype(bf16)


def sum_kernel(parts_ref, out_ref):
    for k in range(NX):
        total = parts_ref[k, 0, :, :].astype(f32)
        for j in range(1, NY):
            total = total + parts_ref[k, j, :, :].astype(f32)
        out_ref[:, k * COLS : (k + 1) * COLS] = total.astype(bf16)


def shape(*dims, dtype=bf16):
    return jax.ShapeDtypeStruct(dims, dtype)


def product(everyone, weight, half):
    depth, wide = weight.shape[2], NY * COLS
    return pl.pallas_call(
        functools.partial(product_kernel, half),
        out_shape=shape(NX, NY, TOK, COLS, dtype=bf16 if half else f32),
        in_specs=[pl.BlockSpec(memory_space=pl.ANY)] * 2,
        scratch_shapes=[
            pltpu.VMEM((NX, NX, TOK, WIDTH // NX), bf16),
            pltpu.VMEM((NX, NZ, depth, wide), bf16),
            pltpu.VMEM((NX, TOK, wide), f32),
            pltpu.SemaphoreType.DMA((2, NX)),
        ],
        name="other" if half else "mine",
        compiler_params=pltpu.CompilerParams(vmem_limit_bytes=52 * 2**20),
        cost_estimate=pl.CostEstimate(
            flops=2 * NX * TOK * WIDTH * wide, bytes_accessed=3 * 10**6, transcendentals=0
        ),
    )(everyone, weight)


def shards(x_input, b_input, c_input, step, log_decay, skip, gain, out_weight):
    depth = out_weight.shape[0]
    core = lax.axis_index("c").astype(jnp.int32)[None]
    swap = pl.pallas_call(
        pack_kernel,
        out_shape=shape(NX, depth, NTP * COLS),
        in_specs=[pl.BlockSpec(memory_space=pltpu.SMEM), pl.BlockSpec(memory_space=pl.ANY)],
        scratch_shapes=[pltpu.VMEM(out_weight.shape, bf16), pltpu.SemaphoreType.DMA(())],
        name="pack",
        compiler_params=pltpu.CompilerParams(vmem_limit_bytes=LARGE),
        cost_estimate=pl.CostEstimate(flops=0, bytes_accessed=3 * 10**5, transcendentals=0),
    )(core, out_weight)
    swap = lax.all_to_all(swap, "x", 0, 0, tiled=True)

    send = call(
        fresh_kernel, shape(CTX, CHUNK + EXTRA, N), 4 * 10**7, 10**6, "fresh", LARGE
    )(x_input, b_input, step, log_decay)
    send, swap = lax.optimization_barrier((send, swap))
    weight = lax.all_gather(swap, "z", axis=0)

    got = lax.all_to_all(send, ("x", "z"), 0, 0, tiled=True)
    inner, scale = call(
        inner_kernel,
        (shape(TOK, WIDTH, dtype=f32), shape(TOK, WIDTH, dtype=f32)),
        10**8,
        2 * 10**6,
        "inner",
    )(x_input, b_input, c_input, step, log_decay, jnp.repeat(skip, P_SIZE)[None])
    entering = call(scan_kernel, shape(CTX, CHUNK, N), 10**6, 7 * 10**5, "scan")(got)
    states = lax.all_to_all(entering, ("x", "z"), 0, 0, tiled=True)

    hidden = call(hidden_kernel, shape(NX, TOK, WIDTH), 3 * 10**7, 2 * 10**6, "hidden")(
        inner, scale, c_input, states, gain[None]
    )
    everyone = lax.all_to_all(hidden, "x", 0, 0, tiled=True)
    other = product(everyone, weight, 1)
    other = lax.ppermute(other, "c", [(0, 1), (1, 0)])
    mine = product(everyone, weight, 0)
    parts = call(pair_kernel, shape(NX, NY, TOK, COLS), 10**6, 2 * 10**6, "pair")(mine, other)
    parts = lax.all_to_all(parts.reshape(NX * NY, TOK, COLS), ("x", "y"), 0, 0, tiled=True)
    return call(sum_kernel, shape(TOK, NX * COLS), 10**6, 10**6, "sum")(
        parts.reshape(NX, NY, TOK, COLS)
    )


def solution(mesh):
    fine = Mesh(mesh.devices.reshape(NX, NZ, NY, NC), ("x", "z", "y", "c"))
    ctx, tp = ("x", "z"), ("y", "c")
    in_specs = (
        P(ctx, tp),
        P(ctx, tp),
        P(ctx, tp),
        P(tp, ctx),
        P(tp, ctx),
        P(tp),
        P(tp),
        P(tp + ctx, None),
    )
    return jax.shard_map(
        shards, mesh=fine, in_specs=in_specs, out_specs=P(ctx, tp), check_vma=False
    )
```

```python
import functools

import jax
import jax.numpy as jnp
from jax import lax
from jax.experimental import pallas as pl
from jax.experimental.pallas import tpu as pltpu
from jax.sharding import Mesh, PartitionSpec as P

NX, NZ, NY, NC = 4, 16, 4, 2
NL = 2
NH = NZ // NL
GROUP = NX * NL
NTP = NY * NC
TOK = 128
HEADS = 16
P_SIZE = 64
N = 128
WIDTH = HEADS * P_SIZE
CTX = NX * NZ
CHUNK = WIDTH // CTX
EXTRA = 8
COLS = 128
QUAD = WIDTH // NX
PART = QUAD // NL
LARGE = 56 * 2**20
f32 = jnp.float32
bf16 = jnp.bfloat16
HIGH = lax.Precision.HIGHEST


def call(kernel, out_shape, flops, moved, name, vmem=32 * 2**20):
    return pl.pallas_call(
        kernel,
        out_shape=out_shape,
        name=name,
        compiler_params=pltpu.CompilerParams(vmem_limit_bytes=vmem),
        cost_estimate=pl.CostEstimate(flops=flops, bytes_accessed=moved, transcendentals=0),
    )


def iota(shape, axis):
    return lax.broadcasted_iota(jnp.int32, shape, axis)


def dot(a, b, ca, cb, precision=None):
    return lax.dot_general(
        a, b, (((ca,), (cb,)), ((), ())), precision=precision, preferred_element_type=f32
    )


def cumulative(logs):
    upto = (iota((TOK, TOK), 0) <= iota((TOK, TOK), 1)).astype(f32)
    return dot(logs, upto, 1, 0, HIGH)


def spread_heads(per_head, head):
    owner = (head == iota((HEADS, WIDTH), 0)).astype(f32)
    return dot(per_head, owner, 0, 0, HIGH)


def sorted_head():
    channel = iota((HEADS, WIDTH), 1)
    return channel // QUAD * (QUAD // P_SIZE) + channel % PART // (P_SIZE // NL)


def sorting():
    to = iota((QUAD, QUAD), 1)
    source = to % PART // 32 * P_SIZE + to % 32 // 16 * 32 + to // PART * 16 + to % 16
    return (iota((QUAD, QUAD), 0) == source).astype(bf16)


def pack_kernel(place_ref, weight_ref, *refs):
    *pieces, held_ref, sem = refs
    copy = pltpu.make_async_copy(weight_ref, held_ref, sem)
    copy.start()
    copy.wait()
    first = place_ref[0] == 0
    me = place_ref[1]
    for k, out_ref in enumerate(pieces):
        x = lax.rem(me + k, NX)
        for y in range(NY):
            even, odd = (
                held_ref[:, pl.ds(pl.multiple_of(((y * NC + c) * NX + x) * COLS, COLS), COLS)]
                for c in range(NC)
            )
            out_ref[:, y * COLS : (y + 1) * COLS] = jnp.where(first, even, odd)
            out_ref[:, (NY + y) * COLS : (NY + y + 1) * COLS] = jnp.where(first, odd, even)


def fresh_kernel(x_ref, b_ref, step_ref, logs_ref, out_ref):
    logs = logs_ref[...]
    cumul = cumulative(logs)
    total = dot(logs, jnp.ones((TOK, TOK), f32), 1, 0, HIGH)
    tail = jnp.exp(total - cumul) * step_ref[...]
    weighted = (x_ref[...].astype(f32) * spread_heads(tail, iota((HEADS, WIDTH), 1) // P_SIZE)).astype(bf16)
    fresh = dot(weighted, b_ref[...], 0, 0).astype(bf16)
    high = total.astype(bf16)
    rest = total - high.astype(f32)
    middle = rest.astype(bf16)
    low = (rest - middle.astype(f32)).astype(bf16)
    row = iota((EXTRA, N), 0)
    for h in range(HEADS):
        first, second, third = (
            jnp.broadcast_to(part[h : h + 1].astype(f32), (EXTRA, N)) for part in (high, middle, low)
        )
        pieces = jnp.where(row == 0, first, jnp.where(row == 1, second, third))
        pieces = jnp.where(row < 3, pieces, 0.0).astype(bf16)
        for k in range(h * P_SIZE // CHUNK, (h + 1) * P_SIZE // CHUNK):
            out_ref[k, :CHUNK, :] = fresh[k * CHUNK : (k + 1) * CHUNK]
            out_ref[k, CHUNK:, :] = pieces


def scan_kernel(got_ref, out_ref):
    state = jnp.zeros((CHUNK, N), f32)
    for k in range(CTX):
        out_ref[k, :, :] = state.astype(bf16)
        pieces = got_ref[k, CHUNK:, :].astype(f32)
        decay = jnp.exp(pieces[0:1] + pieces[1:2] + pieces[2:3])
        state = decay * state + got_ref[k, :CHUNK, :].astype(f32)


def inner_kernel(x_ref, b_ref, c_ref, step_ref, logs_ref, skip_ref, out_ref, scale_ref):
    logs = logs_ref[...]
    cumul = cumulative(logs)
    upto = (iota((TOK, TOK), 1) <= iota((TOK, TOK), 0)).astype(f32)
    cumul_t = dot(upto, logs, 1, 1, HIGH)
    scale_ref[...] = spread_heads(jnp.exp(cumul), sorted_head())
    scores = dot(c_ref[...], b_ref[...], 1, 1)
    within = iota((TOK, TOK), 1) <= iota((TOK, TOK), 0)
    lane_head = iota((TOK, QUAD), 1) % PART // (P_SIZE // NL)
    order = sorting()
    for quad in range(NX):
        columns = slice(quad * QUAD, (quad + 1) * QUAD)
        values = dot(x_ref[:, columns], order, 1, 0).astype(bf16)
        own = skip_ref[:, columns] * values.astype(f32)
        for i in range(QUAD // P_SIZE):
            h = quad * (QUAD // P_SIZE) + i
            spread = cumul_t[:, h : h + 1] - cumul[h : h + 1, :]
            decay = jnp.exp(jnp.where(within, spread, -1e30))
            mixing = (scores * decay * step_ref[h : h + 1, :]).astype(bf16)
            own = own + jnp.where(lane_head == i, dot(mixing, values, 1, 0), 0.0)
        out_ref[:, columns] = own


def hidden_kernel(inner_ref, scale_ref, c_ref, state_ref, gain_ref, out_ref):
    slots = [
        (quad * 4 + i) * 4 + j * NL + parity
        for quad in range(NX)
        for parity in range(NL)
        for i in range(4)
        for j in range(2)
    ]
    states = jnp.concatenate([state_ref[slot] for slot in slots], axis=0)
    ssm = inner_ref[...] + scale_ref[...] * dot(c_ref[...], states, 1, 1)
    meansq = jnp.mean(ssm * ssm, axis=1, keepdims=True)
    hidden = (ssm * lax.rsqrt(meansq + 1e-05) * gain_ref[...]).astype(bf16)
    for quad in range(NX):
        for parity in range(NL):
            begin = quad * QUAD + parity * PART
            part = hidden[:, begin : begin + PART]
            for x in range(NX):
                out_ref[x * NL + parity, :, quad * PART : (quad + 1) * PART] = part


def product_kernel(half, me_ref, hidden_ref, weight_ref, out_ref, tokens_ref, held_ref, sems):
    wide = NY * COLS
    me = me_ref[0]
    copies = []
    for k in range(NX):
        part = hidden_ref.at[:, :, pl.ds(k * PART, PART)]
        rows = weight_ref.at[:, k, :, pl.ds(half * wide, wide)]
        copies.append(pltpu.make_async_copy(part, tokens_ref.at[k], sems.at[0, k]))
        copies.append(pltpu.make_async_copy(rows, held_ref.at[k], sems.at[1, k]))
    for copy in copies:
        copy.start()
    for copy in copies:
        copy.wait()
    low, high = (held_ref[k : k + 2].reshape(2 * PART, wide) for k in (0, 2))
    x = [lax.rem(me + (NX - k), NX) for k in range(NX)]
    for i in range(GROUP):
        left = jnp.concatenate([tokens_ref[x[0], i], tokens_ref[x[1], i]], axis=1)
        right = jnp.concatenate([tokens_ref[x[2], i], tokens_ref[x[3], i]], axis=1)
        term = (dot(left, low, 1, 0) + dot(right, high, 1, 0)).astype(out_ref.dtype)
        for j in range(NY):
            out_ref[i, j, :, :] = term[:, j * COLS : (j + 1) * COLS]


def pair_kernel(mine_ref, other_ref, out_ref):
    out_ref[...] = (mine_ref[...] + other_ref[...].astype(f32)).astype(bf16)


def sum_kernel(parts_ref, out_ref):
    for k in range(NX):
        total = parts_ref[k, 0, :, :].astype(f32)
        for j in range(1, NL * NY):
            total = total + parts_ref[k, j, :, :].astype(f32)
        out_ref[:, k * COLS : (k + 1) * COLS] = total.astype(bf16)


def shape(*dims, dtype=bf16):
    return jax.ShapeDtypeStruct(dims, dtype)


def product(me, everyone, weight, half):
    depth, wide = weight.shape[2], NY * COLS
    return pl.pallas_call(
        functools.partial(product_kernel, half),
        out_shape=shape(GROUP, NY, TOK, COLS, dtype=bf16 if half else f32),
        in_specs=[pl.BlockSpec(memory_space=pltpu.SMEM)] + [pl.BlockSpec(memory_space=pl.ANY)] * 2,
        scratch_shapes=[
            pltpu.VMEM((NX, GROUP, TOK, PART), bf16),
            pltpu.VMEM((NX, NH, depth, wide), bf16),
            pltpu.SemaphoreType.DMA((2, NX)),
        ],
        name="other" if half else "mine",
        compiler_params=pltpu.CompilerParams(vmem_limit_bytes=52 * 2**20),
        cost_estimate=pl.CostEstimate(
            flops=GROUP * TOK * WIDTH * wide, bytes_accessed=3 * 10**6, transcendentals=0
        ),
    )(me, everyone, weight)


def sort_channels(per_channel):
    return per_channel.reshape(NX, 4, 2, NL, 16).transpose(0, 3, 1, 2, 4).reshape(1, WIDTH)


def shards(x_input, b_input, c_input, step, log_decay, skip, gain, out_weight):
    ctx = ("x", "zh", "zl")
    depth = out_weight.shape[0]
    me = lax.axis_index("x").astype(jnp.int32)
    core = lax.axis_index("c").astype(jnp.int32)
    send = call(
        fresh_kernel, shape(CTX, CHUNK + EXTRA, N), 4 * 10**7, 10**6, "fresh", LARGE
    )(x_input, b_input, step, log_decay)
    got = lax.all_to_all(send, ctx, 0, 0, tiled=True)

    out_weight, _ = lax.optimization_barrier((out_weight, send))
    pieces = pl.pallas_call(
        pack_kernel,
        out_shape=(shape(depth, NTP * COLS),) * NX,
        in_specs=[pl.BlockSpec(memory_space=pltpu.SMEM), pl.BlockSpec(memory_space=pl.ANY)],
        scratch_shapes=[pltpu.VMEM(out_weight.shape, bf16), pltpu.SemaphoreType.DMA(())],
        name="pack",
        compiler_params=pltpu.CompilerParams(vmem_limit_bytes=LARGE),
        cost_estimate=pl.CostEstimate(flops=0, bytes_accessed=3 * 10**5, transcendentals=0),
    )(jnp.stack([core, me]), out_weight)
    pieces = [
        lax.ppermute(piece, "x", [(i, (i + k) % NX) for i in range(NX)]) if k else piece
        for k, piece in enumerate(pieces)
    ]
    swap = jnp.stack(pieces)
    weight = lax.all_gather(swap, "zh", axis=0)

    inner, scale = call(
        inner_kernel,
        (shape(TOK, WIDTH, dtype=f32), shape(TOK, WIDTH, dtype=f32)),
        10**8,
        2 * 10**6,
        "inner",
    )(x_input, b_input, c_input, step, log_decay, sort_channels(jnp.repeat(skip, P_SIZE)))
    entering = call(scan_kernel, shape(CTX, CHUNK, N), 10**6, 7 * 10**5, "scan")(got)
    states = lax.all_to_all(entering, ctx, 0, 0, tiled=True)
    states, weight = lax.optimization_barrier((states, weight))

    hidden = call(hidden_kernel, shape(GROUP, TOK, WIDTH // NL), 3 * 10**7, 2 * 10**6, "hidden")(
        inner, scale, c_input, states, sort_channels(gain)
    )
    everyone = lax.all_to_all(hidden, ("x", "zl"), 0, 0, tiled=True)
    other = product(me[None], everyone, weight, 1)
    other = lax.ppermute(other, "c", [(0, 1), (1, 0)])
    mine = product(me[None], everyone, weight, 0)
    parts = call(pair_kernel, shape(GROUP, NY, TOK, COLS), 10**6, 2 * 10**6, "pair")(mine, other)
    parts = parts.reshape(GROUP * NY, TOK, COLS)
    parts = lax.all_to_all(parts, ("x", "zl", "y"), 0, 0, tiled=True)
    return call(sum_kernel, shape(TOK, NX * COLS), 10**6, 10**6, "sum")(
        parts.reshape(NX, NL * NY, TOK, COLS)
    )


def solution(mesh):
    fine = Mesh(mesh.devices.reshape(NX, NH, NL, NY, NC), ("x", "zh", "zl", "y", "c"))
    ctx, tp = ("x", "zh", "zl"), ("y", "c")
    in_specs = (
        P(ctx, tp),
        P(ctx, tp),
        P(ctx, tp),
        P(tp, ctx),
        P(tp, ctx),
        P(tp),
        P(tp),
        P(tp + ctx, None),
    )
    return jax.shard_map(
        shards, mesh=fine, in_specs=in_specs, out_specs=P(ctx, tp), check_vma=False
    )
```

```python
import functools

import jax
import jax.numpy as jnp
from jax import lax
from jax.experimental import pallas as pl
from jax.experimental.pallas import tpu as pltpu
from jax.sharding import Mesh, PartitionSpec as P

NX, NZ, NY, NC = 4, 16, 4, 2
NTP = NY * NC
TOK = 128
HEADS = 16
P_SIZE = 64
N = 128
WIDTH = HEADS * P_SIZE
CTX = NX * NZ
CHUNK = WIDTH // CTX
PAIRS = CHUNK // 2
COLS = 128
LARGE = 56 * 2**20
f32 = jnp.float32
bf16 = jnp.bfloat16
HIGH = lax.Precision.HIGHEST


def call(kernel, out_shape, flops, moved, name, vmem=32 * 2**20):
    return pl.pallas_call(
        kernel,
        out_shape=out_shape,
        name=name,
        compiler_params=pltpu.CompilerParams(vmem_limit_bytes=vmem),
        cost_estimate=pl.CostEstimate(flops=flops, bytes_accessed=moved, transcendentals=0),
    )


def iota(shape, axis):
    return lax.broadcasted_iota(jnp.int32, shape, axis)


def dot(a, b, ca, cb, precision=None):
    return lax.dot_general(
        a, b, (((ca,), (cb,)), ((), ())), precision=precision, preferred_element_type=f32
    )


def cumulative(logs):
    upto = (iota((TOK, TOK), 0) <= iota((TOK, TOK), 1)).astype(f32)
    return dot(logs, upto, 1, 0, HIGH)


def spread_heads(per_head):
    owner = (iota((HEADS, WIDTH), 1) // P_SIZE == iota((HEADS, WIDTH), 0)).astype(f32)
    return dot(per_head, owner, 0, 0, HIGH)


def pack_kernel(core_ref, weight_ref, out_ref, held_ref, sem):
    copy = pltpu.make_async_copy(weight_ref, held_ref, sem)
    copy.start()
    copy.wait()
    first = core_ref[0] == 0
    for x in range(NX):
        for y in range(NY):
            even, odd = (
                held_ref[:, pl.ds(((y * NC + c) * NX + x) * COLS, COLS)] for c in range(NC)
            )
            out_ref[x, :, y * COLS : (y + 1) * COLS] = jnp.where(first, even, odd)
            out_ref[x, :, (NY + y) * COLS : (NY + y + 1) * COLS] = jnp.where(first, odd, even)


def fresh_kernel(x_ref, b_ref, step_ref, logs_ref, out_ref):
    logs = logs_ref[...]
    cumul = cumulative(logs)
    total = dot(logs, jnp.ones((TOK, TOK), f32), 1, 0, HIGH)
    tail = jnp.exp(total - cumul) * step_ref[...]
    weighted = (x_ref[...].astype(f32) * spread_heads(tail)).astype(bf16)
    fresh = dot(weighted, b_ref[...], 0, 0).astype(bf16)
    high = total.astype(bf16)
    low = (total - high.astype(f32)).astype(bf16)
    row = iota((2, N), 0)
    for h in range(HEADS):
        first, second = (jnp.broadcast_to(part[h : h + 1].astype(f32), (2, N)) for part in (high, low))
        pieces = jnp.where(row == 0, first, second).astype(bf16)
        for k in range(h * P_SIZE // CHUNK, (h + 1) * P_SIZE // CHUNK):
            out_ref[k, :PAIRS, :, :] = fresh[k * CHUNK : (k + 1) * CHUNK].reshape(PAIRS, 2, N)
            out_ref[k, PAIRS, :, :] = pieces


def scan_kernel(got_ref, out_ref):
    state = jnp.zeros((CHUNK, N), f32)
    for k in range(CTX):
        out_ref[k, :, :] = state.astype(bf16)
        pieces = got_ref[k, PAIRS, :, :].astype(f32)
        decay = jnp.exp(pieces[0:1] + pieces[1:2])
        state = decay * state + got_ref[k, :PAIRS, :, :].reshape(CHUNK, N).astype(f32)


def inner_kernel(x_ref, b_ref, c_ref, step_ref, logs_ref, skip_ref, out_ref, scale_ref):
    logs = logs_ref[...]
    cumul = cumulative(logs)
    upto = (iota((TOK, TOK), 1) <= iota((TOK, TOK), 0)).astype(f32)
    cumul_t = dot(upto, logs, 1, 1, HIGH)
    scale_ref[...] = spread_heads(jnp.exp(cumul))
    scores = dot(c_ref[...], b_ref[...], 1, 1)
    within = iota((TOK, TOK), 1) <= iota((TOK, TOK), 0)
    left = iota((TOK, 2 * P_SIZE), 1) < P_SIZE
    for pair in range(HEADS // 2):
        columns = slice(pair * 2 * P_SIZE, (pair + 1) * 2 * P_SIZE)
        values = x_ref[:, columns]
        both = []
        for h in (2 * pair, 2 * pair + 1):
            spread = cumul_t[:, h : h + 1] - cumul[h : h + 1, :]
            decay = jnp.exp(jnp.where(within, spread, -1e30))
            mixing = (scores * decay * step_ref[h : h + 1, :]).astype(bf16)
            both.append(dot(mixing, values, 1, 0))
        own = jnp.where(left, both[0], both[1])
        out_ref[:, columns] = own + skip_ref[:, columns] * values.astype(f32)


def hidden_kernel(inner_ref, scale_ref, c_ref, state_ref, gain_ref, out_ref):
    states = state_ref[...].reshape(WIDTH, N)
    ssm = inner_ref[...] + scale_ref[...] * dot(c_ref[...], states, 1, 1)
    meansq = jnp.mean(ssm * ssm, axis=1, keepdims=True)
    hidden = (ssm * lax.rsqrt(meansq + 1e-05) * gain_ref[...]).astype(bf16)
    for k in range(NX):
        out_ref[k, :, :] = hidden


def product_kernel(half, hidden_ref, weight_ref, out_ref, tokens_ref, held_ref, total_ref, sems):
    depth = WIDTH // NX
    wide = NY * COLS
    copies = []
    for k in range(NX):
        part = hidden_ref.at[:, :, pl.ds(k * depth, depth)]
        rows = weight_ref.at[:, k, :, pl.ds(half * wide, wide)]
        copies.append(
            (
                pltpu.make_async_copy(part, tokens_ref.at[k], sems.at[0, k]),
                pltpu.make_async_copy(rows, held_ref.at[k], sems.at[1, k]),
            )
        )
    for pair in copies:
        for copy in pair:
            copy.start()
    for k in range(NX):
        for copy in copies[k]:
            copy.wait()
        rows = held_ref[k].reshape(depth, wide)
        for i in range(NX):
            term = dot(tokens_ref[k, i], rows, 1, 0)
            if k == 0:
                total_ref[i] = term
            elif k < NX - 1:
                total_ref[i] += term
            else:
                term = (total_ref[i] + term).astype(out_ref.dtype)
                for j in range(NY):
                    out_ref[i, j, :, :] = term[:, j * COLS : (j + 1) * COLS]


def pair_kernel(mine_ref, other_ref, out_ref):
    out_ref[...] = (mine_ref[...] + other_ref[...].astype(f32)).astype(bf16)


def sum_kernel(parts_ref, out_ref):
    for k in range(NX):
        total = parts_ref[k, 0, :, :].astype(f32)
        for j in range(1, NY):
            total = total + parts_ref[k, j, :, :].astype(f32)
        out_ref[:, k * COLS : (k + 1) * COLS] = total.astype(bf16)


def shape(*dims, dtype=bf16):
    return jax.ShapeDtypeStruct(dims, dtype)


def product(everyone, weight, half):
    depth, wide = weight.shape[2], NY * COLS
    return pl.pallas_call(
        functools.partial(product_kernel, half),
        out_shape=shape(NX, NY, TOK, COLS, dtype=bf16 if half else f32),
        in_specs=[pl.BlockSpec(memory_space=pl.ANY)] * 2,
        scratch_shapes=[
            pltpu.VMEM((NX, NX, TOK, WIDTH // NX), bf16),
            pltpu.VMEM((NX, NZ, depth, wide), bf16),
            pltpu.VMEM((NX, TOK, wide), f32),
            pltpu.SemaphoreType.DMA((2, NX)),
        ],
        name="other" if half else "mine",
        compiler_params=pltpu.CompilerParams(vmem_limit_bytes=52 * 2**20),
        cost_estimate=pl.CostEstimate(
            flops=2 * NX * TOK * WIDTH * wide, bytes_accessed=3 * 10**6, transcendentals=0
        ),
    )(everyone, weight)


def shards(x_input, b_input, c_input, step, log_decay, skip, gain, out_weight):
    depth = out_weight.shape[0]
    core = lax.axis_index("c").astype(jnp.int32)[None]
    swap = pl.pallas_call(
        pack_kernel,
        out_shape=shape(NX, depth, NTP * COLS),
        in_specs=[pl.BlockSpec(memory_space=pltpu.SMEM), pl.BlockSpec(memory_space=pl.ANY)],
        scratch_shapes=[pltpu.VMEM(out_weight.shape, bf16), pltpu.SemaphoreType.DMA(())],
        name="pack",
        compiler_params=pltpu.CompilerParams(vmem_limit_bytes=LARGE),
        cost_estimate=pl.CostEstimate(flops=0, bytes_accessed=3 * 10**5, transcendentals=0),
    )(core, out_weight)
    swap = lax.all_to_all(swap, "x", 0, 0, tiled=True)

    send = call(
        fresh_kernel, shape(CTX, PAIRS + 1, 2, N), 4 * 10**7, 10**6, "fresh", LARGE
    )(x_input, b_input, step, log_decay)
    send, swap = lax.optimization_barrier((send, swap))
    weight = lax.all_gather(swap, "z", axis=0)

    got = lax.all_to_all(send, ("x", "z"), 0, 0, tiled=True)
    inner, scale = call(
        inner_kernel,
        (shape(TOK, WIDTH, dtype=f32), shape(TOK, WIDTH, dtype=f32)),
        10**8,
        2 * 10**6,
        "inner",
    )(x_input, b_input, c_input, step, log_decay, jnp.repeat(skip, P_SIZE)[None])
    entering = call(scan_kernel, shape(CTX, CHUNK, N), 10**6, 7 * 10**5, "scan")(got)
    states = lax.all_to_all(entering, ("x", "z"), 0, 0, tiled=True)

    hidden = call(hidden_kernel, shape(NX, TOK, WIDTH), 3 * 10**7, 2 * 10**6, "hidden")(
        inner, scale, c_input, states, gain[None]
    )
    everyone = lax.all_to_all(hidden, "x", 0, 0, tiled=True)
    other = product(everyone, weight, 1)
    other = lax.ppermute(other, "c", [(0, 1), (1, 0)])
    mine = product(everyone, weight, 0)
    parts = call(pair_kernel, shape(NX, NY, TOK, COLS), 10**6, 2 * 10**6, "pair")(mine, other)
    parts = lax.all_to_all(parts.reshape(NX * NY, TOK, COLS), ("x", "y"), 0, 0, tiled=True)
    return call(sum_kernel, shape(TOK, NX * COLS), 10**6, 10**6, "sum")(
        parts.reshape(NX, NY, TOK, COLS)
    )


def solution(mesh):
    fine = Mesh(mesh.devices.reshape(NX, NZ, NY, NC), ("x", "z", "y", "c"))
    ctx, tp = ("x", "z"), ("y", "c")
    in_specs = (
        P(ctx, tp),
        P(ctx, tp),
        P(ctx, tp),
        P(tp, ctx),
        P(tp, ctx),
        P(tp),
        P(tp),
        P(tp + ctx, None),
    )
    return jax.shard_map(
        shards, mesh=fine, in_specs=in_specs, out_specs=P(ctx, tp), check_vma=False
    )
```

```python
import functools

import jax
import jax.numpy as jnp
from jax import lax
from jax.experimental import pallas as pl
from jax.experimental.pallas import tpu as pltpu
from jax.sharding import Mesh, PartitionSpec as P

NX, NZ, NY, NC = 4, 16, 4, 2
NTP = NY * NC
TOK = 128
HEADS = 16
P_SIZE = 64
N = 128
WIDTH = HEADS * P_SIZE
CTX = NX * NZ
CHUNK = WIDTH // CTX
PAIRS = CHUNK // 2
COLS = 128
LARGE = 56 * 2**20
f32 = jnp.float32
bf16 = jnp.bfloat16
HIGH = lax.Precision.HIGHEST


def call(kernel, out_shape, flops, moved, name, vmem=32 * 2**20):
    return pl.pallas_call(
        kernel,
        out_shape=out_shape,
        name=name,
        compiler_params=pltpu.CompilerParams(vmem_limit_bytes=vmem),
        cost_estimate=pl.CostEstimate(flops=flops, bytes_accessed=moved, transcendentals=0),
    )


def iota(shape, axis):
    return lax.broadcasted_iota(jnp.int32, shape, axis)


def dot(a, b, ca, cb, precision=None):
    return lax.dot_general(
        a, b, (((ca,), (cb,)), ((), ())), precision=precision, preferred_element_type=f32
    )


def cumulative(logs):
    upto = (iota((TOK, TOK), 0) <= iota((TOK, TOK), 1)).astype(f32)
    return dot(logs, upto, 1, 0, HIGH)


def spread_heads(per_head):
    owner = (iota((HEADS, WIDTH), 1) // P_SIZE == iota((HEADS, WIDTH), 0)).astype(f32)
    return dot(per_head, owner, 0, 0, HIGH)


def pack_kernel(core_ref, held_ref, out_ref):
    first = core_ref[0] == 0
    for x in range(NX):
        for y in range(NY):
            even, odd = (
                held_ref[:, pl.ds(((y * NC + c) * NX + x) * COLS, COLS)] for c in range(NC)
            )
            out_ref[x, :, y * COLS : (y + 1) * COLS] = jnp.where(first, even, odd)
            out_ref[x, :, (NY + y) * COLS : (NY + y + 1) * COLS] = jnp.where(first, odd, even)


def fresh_kernel(x_ref, b_ref, step_ref, logs_ref, out_ref):
    logs = logs_ref[...]
    cumul = cumulative(logs)
    total = dot(logs, jnp.ones((TOK, TOK), f32), 1, 0, HIGH)
    tail = jnp.exp(total - cumul) * step_ref[...]
    weighted = (x_ref[...].astype(f32) * spread_heads(tail)).astype(bf16)
    fresh = dot(weighted, b_ref[...], 0, 0).astype(bf16)
    high = total.astype(bf16)
    low = (total - high.astype(f32)).astype(bf16)
    row = iota((2, N), 0)
    for h in range(HEADS):
        first, second = (jnp.broadcast_to(part[h : h + 1].astype(f32), (2, N)) for part in (high, low))
        pieces = jnp.where(row == 0, first, second).astype(bf16)
        for k in range(h * P_SIZE // CHUNK, (h + 1) * P_SIZE // CHUNK):
            out_ref[k, :PAIRS, :, :] = fresh[k * CHUNK : (k + 1) * CHUNK].reshape(PAIRS, 2, N)
            out_ref[k, PAIRS, :, :] = pieces


def scan_kernel(got_ref, out_ref):
    state = jnp.zeros((CHUNK, N), f32)
    for k in range(CTX):
        out_ref[k, :, :] = state.astype(bf16)
        pieces = got_ref[k, PAIRS, :, :].astype(f32)
        decay = jnp.exp(pieces[0:1] + pieces[1:2])
        state = decay * state + got_ref[k, :PAIRS, :, :].reshape(CHUNK, N).astype(f32)


def inner_kernel(x_ref, b_ref, c_ref, step_ref, logs_ref, skip_ref, out_ref, scale_ref):
    logs = logs_ref[...]
    cumul = cumulative(logs)
    upto = (iota((TOK, TOK), 1) <= iota((TOK, TOK), 0)).astype(f32)
    cumul_t = dot(upto, logs, 1, 1, HIGH)
    scale_ref[...] = spread_heads(jnp.exp(cumul))
    scores = dot(c_ref[...], b_ref[...], 1, 1)
    within = iota((TOK, TOK), 1) <= iota((TOK, TOK), 0)
    left = iota((TOK, 2 * P_SIZE), 1) < P_SIZE
    for pair in range(HEADS // 2):
        columns = slice(pair * 2 * P_SIZE, (pair + 1) * 2 * P_SIZE)
        values = x_ref[:, columns]
        both = []
        for h in (2 * pair, 2 * pair + 1):
            spread = cumul_t[:, h : h + 1] - cumul[h : h + 1, :]
            decay = jnp.exp(jnp.where(within, spread, -1e30))
            mixing = (scores * decay * step_ref[h : h + 1, :]).astype(bf16)
            both.append(dot(mixing, values, 1, 0))
        own = jnp.where(left, both[0], both[1])
        out_ref[:, columns] = own + skip_ref[:, columns] * values.astype(f32)


def hidden_kernel(inner_ref, scale_ref, c_ref, state_ref, gain_ref, out_ref):
    states = state_ref[...].reshape(WIDTH, N)
    ssm = inner_ref[...] + scale_ref[...] * dot(c_ref[...], states, 1, 1)
    meansq = jnp.mean(ssm * ssm, axis=1, keepdims=True)
    hidden = (ssm * lax.rsqrt(meansq + 1e-05) * gain_ref[...]).astype(bf16)
    for k in range(NX):
        out_ref[k, :, :] = hidden


def product_kernel(half, hidden_ref, weight_ref, out_ref, held_ref, total_ref, sems):
    depth = WIDTH // NX
    wide = NY * COLS
    copies = [
        pltpu.make_async_copy(
            weight_ref.at[:, k, :, pl.ds(half * wide, wide)], held_ref.at[k], sems.at[k]
        )
        for k in range(NX)
    ]
    for copy in copies:
        copy.start()
    for k in range(NX):
        copies[k].wait()
        rows = held_ref[k].reshape(depth, wide)
        for i in range(NX):
            term = dot(hidden_ref[i, :, k * depth : (k + 1) * depth], rows, 1, 0)
            if k == 0:
                total_ref[i] = term
            elif k < NX - 1:
                total_ref[i] += term
            else:
                term = (total_ref[i] + term).astype(out_ref.dtype)
                for j in range(NY):
                    out_ref[i, j, :, :] = term[:, j * COLS : (j + 1) * COLS]


def pair_kernel(mine_ref, other_ref, out_ref):
    out_ref[...] = (mine_ref[...] + other_ref[...].astype(f32)).astype(bf16)


def sum_kernel(parts_ref, out_ref):
    for k in range(NX):
        total = parts_ref[k, 0, :, :].astype(f32)
        for j in range(1, NY):
            total = total + parts_ref[k, j, :, :].astype(f32)
        out_ref[:, k * COLS : (k + 1) * COLS] = total.astype(bf16)


def shape(*dims, dtype=bf16):
    return jax.ShapeDtypeStruct(dims, dtype)


def product(everyone, weight, half):
    depth, wide = weight.shape[2], NY * COLS
    return pl.pallas_call(
        functools.partial(product_kernel, half),
        out_shape=shape(NX, NY, TOK, COLS, dtype=bf16 if half else f32),
        in_specs=[pl.BlockSpec(memory_space=pltpu.VMEM), pl.BlockSpec(memory_space=pl.ANY)],
        scratch_shapes=[
            pltpu.VMEM((NX, NZ, depth, wide), bf16),
            pltpu.VMEM((NX, TOK, wide), f32),
            pltpu.SemaphoreType.DMA((NX,)),
        ],
        name="other" if half else "mine",
        compiler_params=pltpu.CompilerParams(vmem_limit_bytes=103 * 2**19),
        cost_estimate=pl.CostEstimate(
            flops=2 * NX * TOK * WIDTH * wide, bytes_accessed=3 * 10**6, transcendentals=0
        ),
    )(everyone, weight)


def shards(x_input, b_input, c_input, step, log_decay, skip, gain, out_weight):
    depth = out_weight.shape[0]
    core = lax.axis_index("c").astype(jnp.int32)[None]
    swap = pl.pallas_call(
        pack_kernel,
        out_shape=shape(NX, depth, NTP * COLS),
        in_specs=[pl.BlockSpec(memory_space=pltpu.SMEM), pl.BlockSpec(memory_space=pltpu.VMEM)],
        name="pack",
        compiler_params=pltpu.CompilerParams(vmem_limit_bytes=32 * 2**20),
        cost_estimate=pl.CostEstimate(flops=0, bytes_accessed=3 * 10**5, transcendentals=0),
    )(core, out_weight)
    swap = lax.all_to_all(swap, "x", 0, 0, tiled=True)

    send = call(
        fresh_kernel, shape(CTX, PAIRS + 1, 2, N), 4 * 10**7, 10**6, "fresh", LARGE
    )(x_input, b_input, step, log_decay)
    send, swap = lax.optimization_barrier((send, swap))
    flat = swap.reshape(NX, 2, 8, NTP, COLS).transpose(2, 0, 1, 3, 4).reshape(8, NX * 2 * NTP * COLS)
    weight = lax.all_gather(flat, "z", axis=0).reshape(NZ, 8, NX, 2, NTP, COLS)
    weight = weight.transpose(0, 2, 3, 1, 4, 5).reshape(NZ, NX, depth, NTP * COLS)

    got = lax.all_to_all(send, ("x", "z"), 0, 0, tiled=True)
    inner, scale = call(
        inner_kernel,
        (shape(TOK, WIDTH, dtype=f32), shape(TOK, WIDTH, dtype=f32)),
        10**8,
        2 * 10**6,
        "inner",
    )(x_input, b_input, c_input, step, log_decay, jnp.repeat(skip, P_SIZE)[None])
    entering = call(scan_kernel, shape(CTX, CHUNK, N), 10**6, 7 * 10**5, "scan")(got)
    states = lax.all_to_all(entering, ("x", "z"), 0, 0, tiled=True)

    hidden = call(hidden_kernel, shape(NX, TOK, WIDTH), 3 * 10**7, 2 * 10**6, "hidden")(
        inner, scale, c_input, states, gain[None]
    )
    everyone = lax.all_to_all(hidden, "x", 0, 0, tiled=True)
    other = product(everyone, weight, 1)
    other = lax.ppermute(other, "c", [(0, 1), (1, 0)])
    mine = product(everyone, weight, 0)
    parts = call(pair_kernel, shape(NX, NY, TOK, COLS), 10**6, 2 * 10**6, "pair")(mine, other)
    parts = lax.all_to_all(parts.reshape(NX * NY, TOK, COLS), ("x", "y"), 0, 0, tiled=True)
    return call(sum_kernel, shape(TOK, NX * COLS), 10**6, 10**6, "sum")(
        parts.reshape(NX, NY, TOK, COLS)
    )


def solution(mesh):
    fine = Mesh(mesh.devices.reshape(NX, NZ, NY, NC), ("x", "z", "y", "c"))
    ctx, tp = ("x", "z"), ("y", "c")
    in_specs = (
        P(ctx, tp),
        P(ctx, tp),
        P(ctx, tp),
        P(tp, ctx),
        P(tp, ctx),
        P(tp),
        P(tp),
        P(tp + ctx, None),
    )
    return jax.shard_map(
        shards, mesh=fine, in_specs=in_specs, out_specs=P(ctx, tp), check_vma=False
    )
```

```python
import functools

import jax
import jax.numpy as jnp
from jax import lax
from jax.experimental import pallas as pl
from jax.experimental.pallas import tpu as pltpu
from jax.sharding import Mesh, PartitionSpec as P

NX, NZ, NY, NC = 4, 16, 4, 2
NTP = NY * NC
TOK = 128
HEADS = 16
P_SIZE = 64
N = 128
WIDTH = HEADS * P_SIZE
CTX = NX * NZ
CHUNK = WIDTH // CTX
PAIRS = CHUNK // 2
COLS = 128
LARGE = 56 * 2**20
f32 = jnp.float32
bf16 = jnp.bfloat16
HIGH = lax.Precision.HIGHEST


def call(kernel, out_shape, flops, moved, name, vmem=32 * 2**20):
    return pl.pallas_call(
        kernel,
        out_shape=out_shape,
        name=name,
        compiler_params=pltpu.CompilerParams(vmem_limit_bytes=vmem),
        cost_estimate=pl.CostEstimate(flops=flops, bytes_accessed=moved, transcendentals=0),
    )


def iota(shape, axis):
    return lax.broadcasted_iota(jnp.int32, shape, axis)


def dot(a, b, ca, cb, precision=None):
    return lax.dot_general(
        a, b, (((ca,), (cb,)), ((), ())), precision=precision, preferred_element_type=f32
    )


def cumulative(logs):
    upto = (iota((TOK, TOK), 0) <= iota((TOK, TOK), 1)).astype(f32)
    return dot(logs, upto, 1, 0, HIGH)


def spread_heads(per_head):
    owner = (iota((HEADS, WIDTH), 1) // P_SIZE == iota((HEADS, WIDTH), 0)).astype(f32)
    return dot(per_head, owner, 0, 0, HIGH)


def pack_kernel(weight_ref, out_ref):
    for x in range(NX):
        for c in range(NC):
            for y in range(NY):
                begin = ((y * NC + c) * NX + x) * COLS
                end = (c * NY + y) * COLS
                out_ref[x, :, end : end + COLS] = weight_ref[:, begin : begin + COLS]


def fresh_kernel(x_ref, b_ref, step_ref, logs_ref, out_ref):
    logs = logs_ref[...]
    cumul = cumulative(logs)
    total = dot(logs, jnp.ones((TOK, TOK), f32), 1, 0, HIGH)
    tail = jnp.exp(total - cumul) * step_ref[...]
    weighted = (x_ref[...].astype(f32) * spread_heads(tail)).astype(bf16)
    fresh = dot(weighted, b_ref[...], 0, 0).astype(bf16)
    high = total.astype(bf16)
    low = (total - high.astype(f32)).astype(bf16)
    row = iota((2, N), 0)
    for h in range(HEADS):
        first, second = (jnp.broadcast_to(part[h : h + 1].astype(f32), (2, N)) for part in (high, low))
        pieces = jnp.where(row == 0, first, second).astype(bf16)
        for k in range(h * P_SIZE // CHUNK, (h + 1) * P_SIZE // CHUNK):
            out_ref[k, :PAIRS, :, :] = fresh[k * CHUNK : (k + 1) * CHUNK].reshape(PAIRS, 2, N)
            out_ref[k, PAIRS, :, :] = pieces


def scan_kernel(got_ref, out_ref):
    state = jnp.zeros((CHUNK, N), f32)
    for k in range(CTX):
        out_ref[k, :, :] = state.astype(bf16)
        pieces = got_ref[k, PAIRS, :, :].astype(f32)
        decay = jnp.exp(pieces[0:1] + pieces[1:2])
        state = decay * state + got_ref[k, :PAIRS, :, :].reshape(CHUNK, N).astype(f32)


def inner_kernel(x_ref, b_ref, c_ref, step_ref, logs_ref, skip_ref, out_ref, scale_ref):
    logs = logs_ref[...]
    cumul = cumulative(logs)
    upto = (iota((TOK, TOK), 1) <= iota((TOK, TOK), 0)).astype(f32)
    cumul_t = dot(upto, logs, 1, 1, HIGH)
    scale_ref[...] = spread_heads(jnp.exp(cumul))
    scores = dot(c_ref[...], b_ref[...], 1, 1)
    within = iota((TOK, TOK), 1) <= iota((TOK, TOK), 0)
    left = iota((TOK, 2 * P_SIZE), 1) < P_SIZE
    for pair in range(HEADS // 2):
        columns = slice(pair * 2 * P_SIZE, (pair + 1) * 2 * P_SIZE)
        values = x_ref[:, columns]
        both = []
        for h in (2 * pair, 2 * pair + 1):
            spread = cumul_t[:, h : h + 1] - cumul[h : h + 1, :]
            decay = jnp.exp(jnp.where(within, spread, -1e30))
            mixing = (scores * decay * step_ref[h : h + 1, :]).astype(bf16)
            both.append(dot(mixing, values, 1, 0))
        own = jnp.where(left, both[0], both[1])
        out_ref[:, columns] = own + skip_ref[:, columns] * values.astype(f32)


def hidden_kernel(inner_ref, scale_ref, c_ref, state_ref, gain_ref, out_ref):
    states = state_ref[...].reshape(WIDTH, N)
    ssm = inner_ref[...] + scale_ref[...] * dot(c_ref[...], states, 1, 1)
    meansq = jnp.mean(ssm * ssm, axis=1, keepdims=True)
    hidden = (ssm * lax.rsqrt(meansq + 1e-05) * gain_ref[...]).astype(bf16)
    for k in range(NX):
        out_ref[k, :, :] = hidden


def product_kernel(half, core_ref, hidden_ref, weight_ref, out_ref, held_ref, total_ref, sems):
    depth = WIDTH // NX
    wide = NY * COLS
    core = 1 - core_ref[0] if half else core_ref[0]
    begin = pl.multiple_of(core * wide, wide)
    copies = [
        pltpu.make_async_copy(
            weight_ref.at[:, k, :, pl.ds(begin, wide)], held_ref.at[k], sems.at[k]
        )
        for k in range(NX)
    ]
    for copy in copies:
        copy.start()
    for k in range(NX):
        copies[k].wait()
        rows = held_ref[k].reshape(depth, wide)
        for i in range(NX):
            term = dot(hidden_ref[i, :, k * depth : (k + 1) * depth], rows, 1, 0)
            if k == 0:
                total_ref[i] = term
            elif k < NX - 1:
                total_ref[i] += term
            else:
                term = (total_ref[i] + term).astype(out_ref.dtype)
                for j in range(NY):
                    out_ref[i, j, :, :] = term[:, j * COLS : (j + 1) * COLS]


def pair_kernel(mine_ref, other_ref, out_ref):
    out_ref[...] = (mine_ref[...] + other_ref[...].astype(f32)).astype(bf16)


def sum_kernel(parts_ref, out_ref):
    for k in range(NX):
        total = parts_ref[k, 0, :, :].astype(f32)
        for j in range(1, NY):
            total = total + parts_ref[k, j, :, :].astype(f32)
        out_ref[:, k * COLS : (k + 1) * COLS] = total.astype(bf16)


def shape(*dims, dtype=bf16):
    return jax.ShapeDtypeStruct(dims, dtype)


def product(core, everyone, weight, half):
    depth, wide = weight.shape[2], NY * COLS
    return pl.pallas_call(
        functools.partial(product_kernel, half),
        out_shape=shape(NX, NY, TOK, COLS, dtype=bf16 if half else f32),
        in_specs=[
            pl.BlockSpec(memory_space=pltpu.SMEM),
            pl.BlockSpec(memory_space=pltpu.VMEM),
            pl.BlockSpec(memory_space=pl.ANY),
        ],
        scratch_shapes=[
            pltpu.VMEM((NX, NZ, depth, wide), bf16),
            pltpu.VMEM((NX, TOK, wide), f32),
            pltpu.SemaphoreType.DMA((NX,)),
        ],
        name="other" if half else "mine",
        compiler_params=pltpu.CompilerParams(vmem_limit_bytes=103 * 2**19),
        cost_estimate=pl.CostEstimate(
            flops=2 * NX * TOK * WIDTH * wide, bytes_accessed=3 * 10**6, transcendentals=0
        ),
    )(core, everyone, weight)


def shards(x_input, b_input, c_input, step, log_decay, skip, gain, out_weight):
    depth = out_weight.shape[0]
    core = lax.axis_index("c").astype(jnp.int32)[None]
    swap = pl.pallas_call(
        pack_kernel,
        out_shape=shape(NX, depth, NTP * COLS),
        name="pack",
        compiler_params=pltpu.CompilerParams(vmem_limit_bytes=32 * 2**20),
        cost_estimate=pl.CostEstimate(flops=0, bytes_accessed=3 * 10**5, transcendentals=0),
    )(out_weight)
    swap = lax.all_to_all(swap, "x", 0, 0, tiled=True)

    send = call(
        fresh_kernel, shape(CTX, PAIRS + 1, 2, N), 4 * 10**7, 10**6, "fresh", LARGE
    )(x_input, b_input, step, log_decay)
    send, swap = lax.optimization_barrier((send, swap))
    flat = swap.reshape(NX, 2, 8, NTP, COLS).transpose(2, 0, 1, 3, 4).reshape(8, NX * 2 * NTP * COLS)
    weight = lax.all_gather(flat, "z", axis=0).reshape(NZ, 8, NX, 2, NTP, COLS)
    weight = weight.transpose(0, 2, 3, 1, 4, 5).reshape(NZ, NX, depth, NTP * COLS)

    got = lax.all_to_all(send, ("x", "z"), 0, 0, tiled=True)
    inner, scale = call(
        inner_kernel,
        (shape(TOK, WIDTH, dtype=f32), shape(TOK, WIDTH, dtype=f32)),
        10**8,
        2 * 10**6,
        "inner",
    )(x_input, b_input, c_input, step, log_decay, jnp.repeat(skip, P_SIZE)[None])
    entering = call(scan_kernel, shape(CTX, CHUNK, N), 10**6, 7 * 10**5, "scan")(got)
    states = lax.all_to_all(entering, ("x", "z"), 0, 0, tiled=True)

    hidden = call(hidden_kernel, shape(NX, TOK, WIDTH), 3 * 10**7, 2 * 10**6, "hidden")(
        inner, scale, c_input, states, gain[None]
    )
    everyone = lax.all_to_all(hidden, "x", 0, 0, tiled=True)
    other = product(core, everyone, weight, 1)
    other = lax.ppermute(other, "c", [(0, 1), (1, 0)])
    mine = product(core, everyone, weight, 0)
    parts = call(pair_kernel, shape(NX, NY, TOK, COLS), 10**6, 2 * 10**6, "pair")(mine, other)
    parts = lax.all_to_all(parts.reshape(NX * NY, TOK, COLS), ("x", "y"), 0, 0, tiled=True)
    return call(sum_kernel, shape(TOK, NX * COLS), 10**6, 10**6, "sum")(
        parts.reshape(NX, NY, TOK, COLS)
    )


def solution(mesh):
    fine = Mesh(mesh.devices.reshape(NX, NZ, NY, NC), ("x", "z", "y", "c"))
    ctx, tp = ("x", "z"), ("y", "c")
    in_specs = (
        P(ctx, tp),
        P(ctx, tp),
        P(ctx, tp),
        P(tp, ctx),
        P(tp, ctx),
        P(tp),
        P(tp),
        P(tp + ctx, None),
    )
    return jax.shard_map(
        shards, mesh=fine, in_specs=in_specs, out_specs=P(ctx, tp), check_vma=False
    )
```

```python
import functools

import jax
import jax.numpy as jnp
from jax import lax
from jax.experimental import pallas as pl
from jax.experimental.pallas import tpu as pltpu
from jax.sharding import Mesh, PartitionSpec as P

NX, NZ, NY, NC = 4, 16, 4, 2
NTP = NY * NC
TOK = 128
HEADS = 16
P_SIZE = 64
N = 128
WIDTH = HEADS * P_SIZE
CTX = NX * NZ
CHUNK = WIDTH // CTX
PAIRS = CHUNK // 2
COLS = 128
LARGE = 56 * 2**20
f32 = jnp.float32
bf16 = jnp.bfloat16
HIGH = lax.Precision.HIGHEST


def call(kernel, out_shape, flops, moved, name, vmem=32 * 2**20):
    return pl.pallas_call(
        kernel,
        out_shape=out_shape,
        name=name,
        compiler_params=pltpu.CompilerParams(vmem_limit_bytes=vmem),
        cost_estimate=pl.CostEstimate(flops=flops, bytes_accessed=moved, transcendentals=0),
    )


def iota(shape, axis):
    return lax.broadcasted_iota(jnp.int32, shape, axis)


def dot(a, b, ca, cb, precision=None):
    return lax.dot_general(
        a, b, (((ca,), (cb,)), ((), ())), precision=precision, preferred_element_type=f32
    )


def cumulative(logs):
    upto = (iota((TOK, TOK), 0) <= iota((TOK, TOK), 1)).astype(f32)
    return dot(logs, upto, 1, 0, HIGH)


def spread_heads(per_head):
    owner = (iota((HEADS, WIDTH), 1) // P_SIZE == iota((HEADS, WIDTH), 0)).astype(f32)
    return dot(per_head, owner, 0, 0, HIGH)


def pack_kernel(core_ref, held_ref, out_ref):
    first = core_ref[0] == 0
    for x in range(NX):
        for y in range(NY):
            even, odd = (
                held_ref[:, pl.ds(((y * NC + c) * NX + x) * COLS, COLS)] for c in range(NC)
            )
            out_ref[x, :, y * COLS : (y + 1) * COLS] = jnp.where(first, even, odd)
            out_ref[x, :, (NY + y) * COLS : (NY + y + 1) * COLS] = jnp.where(first, odd, even)


def fresh_kernel(x_ref, b_ref, step_ref, logs_ref, out_ref):
    logs = logs_ref[...]
    cumul = cumulative(logs)
    total = dot(logs, jnp.ones((TOK, TOK), f32), 1, 0, HIGH)
    tail = jnp.exp(total - cumul) * step_ref[...]
    weighted = (x_ref[...].astype(f32) * spread_heads(tail)).astype(bf16)
    fresh = dot(weighted, b_ref[...], 0, 0).astype(bf16)
    high = total.astype(bf16)
    low = (total - high.astype(f32)).astype(bf16)
    row = iota((2, N), 0)
    for h in range(HEADS):
        first, second = (jnp.broadcast_to(part[h : h + 1].astype(f32), (2, N)) for part in (high, low))
        pieces = jnp.where(row == 0, first, second).astype(bf16)
        for k in range(h * P_SIZE // CHUNK, (h + 1) * P_SIZE // CHUNK):
            out_ref[k, :PAIRS, :, :] = fresh[k * CHUNK : (k + 1) * CHUNK].reshape(PAIRS, 2, N)
            out_ref[k, PAIRS, :, :] = pieces


def scan_kernel(got_ref, out_ref):
    state = jnp.zeros((CHUNK, N), f32)
    pieces = got_ref[:, PAIRS, :, :].astype(f32)
    decays = jnp.exp(pieces[:, 0, :] + pieces[:, 1, :])
    for k in range(CTX):
        out_ref[k, :, :] = state.astype(bf16)
        state = decays[k : k + 1] * state + got_ref[k, :PAIRS, :, :].reshape(CHUNK, N).astype(f32)


def inner_kernel(x_ref, b_ref, c_ref, step_ref, logs_ref, skip_ref, out_ref, scale_ref):
    logs = logs_ref[...]
    cumul = cumulative(logs)
    upto = (iota((TOK, TOK), 1) <= iota((TOK, TOK), 0)).astype(f32)
    cumul_t = dot(upto, logs, 1, 1, HIGH)
    scale_ref[...] = spread_heads(jnp.exp(cumul))
    scores = dot(c_ref[...], b_ref[...], 1, 1)
    within = iota((TOK, TOK), 1) <= iota((TOK, TOK), 0)
    left = iota((TOK, 2 * P_SIZE), 1) < P_SIZE
    for pair in range(HEADS // 2):
        columns = slice(pair * 2 * P_SIZE, (pair + 1) * 2 * P_SIZE)
        values = x_ref[:, columns]
        both = []
        for h in (2 * pair, 2 * pair + 1):
            spread = cumul_t[:, h : h + 1] - cumul[h : h + 1, :]
            decay = jnp.exp(jnp.where(within, spread, -1e30))
            mixing = (scores * decay * step_ref[h : h + 1, :]).astype(bf16)
            both.append(dot(mixing, values, 1, 0))
        own = jnp.where(left, both[0], both[1])
        out_ref[:, columns] = own + skip_ref[:, columns] * values.astype(f32)


def hidden_kernel(inner_ref, scale_ref, c_ref, state_ref, gain_ref, out_ref):
    states = state_ref[...].reshape(WIDTH, N)
    ssm = inner_ref[...] + scale_ref[...] * dot(c_ref[...], states, 1, 1)
    meansq = jnp.mean(ssm * ssm, axis=1, keepdims=True)
    hidden = (ssm * lax.rsqrt(meansq + 1e-05) * gain_ref[...]).astype(bf16)
    for k in range(NX):
        out_ref[k, :, :] = hidden


def product_kernel(half, hidden_ref, weight_ref, out_ref, held_ref, total_ref, sems):
    depth = WIDTH // NX
    wide = NY * COLS
    copies = [
        pltpu.make_async_copy(
            weight_ref.at[:, k, :, pl.ds(half * wide, wide)], held_ref.at[k], sems.at[k]
        )
        for k in range(NX)
    ]
    for copy in copies:
        copy.start()
    for k in range(NX):
        copies[k].wait()
        rows = held_ref[k].reshape(depth, wide)
        for i in range(NX):
            term = dot(hidden_ref[i, :, k * depth : (k + 1) * depth], rows, 1, 0)
            if k == 0:
                total_ref[i] = term
            elif k < NX - 1:
                total_ref[i] += term
            else:
                term = (total_ref[i] + term).astype(out_ref.dtype)
                for j in range(NY):
                    out_ref[i, j, :, :] = term[:, j * COLS : (j + 1) * COLS]


def pair_kernel(mine_ref, other_ref, out_ref):
    out_ref[...] = (mine_ref[...] + other_ref[...].astype(f32)).astype(bf16)


def sum_kernel(parts_ref, out_ref):
    for k in range(NX):
        total = parts_ref[k, 0, :, :].astype(f32)
        for j in range(1, NY):
            total = total + parts_ref[k, j, :, :].astype(f32)
        out_ref[:, k * COLS : (k + 1) * COLS] = total.astype(bf16)


def shape(*dims, dtype=bf16):
    return jax.ShapeDtypeStruct(dims, dtype)


def product(everyone, weight, half):
    depth, wide = weight.shape[2], NY * COLS
    return pl.pallas_call(
        functools.partial(product_kernel, half),
        out_shape=shape(NX, NY, TOK, COLS, dtype=bf16 if half else f32),
        in_specs=[pl.BlockSpec(memory_space=pltpu.VMEM), pl.BlockSpec(memory_space=pl.ANY)],
        scratch_shapes=[
            pltpu.VMEM((NX, NZ, depth, wide), bf16),
            pltpu.VMEM((NX, TOK, wide), f32),
            pltpu.SemaphoreType.DMA((NX,)),
        ],
        name="other" if half else "mine",
        compiler_params=pltpu.CompilerParams(vmem_limit_bytes=103 * 2**19),
        cost_estimate=pl.CostEstimate(
            flops=2 * NX * TOK * WIDTH * wide, bytes_accessed=3 * 10**6, transcendentals=0
        ),
    )(everyone, weight)


def shards(x_input, b_input, c_input, step, log_decay, skip, gain, out_weight):
    depth = out_weight.shape[0]
    core = lax.axis_index("c").astype(jnp.int32)[None]
    swap = pl.pallas_call(
        pack_kernel,
        out_shape=shape(NX, depth, NTP * COLS),
        in_specs=[pl.BlockSpec(memory_space=pltpu.SMEM), pl.BlockSpec(memory_space=pltpu.VMEM)],
        name="pack",
        compiler_params=pltpu.CompilerParams(vmem_limit_bytes=32 * 2**20),
        cost_estimate=pl.CostEstimate(flops=0, bytes_accessed=3 * 10**5, transcendentals=0),
    )(core, out_weight)
    swap = lax.all_to_all(swap, "x", 0, 0, tiled=True)

    send = call(
        fresh_kernel, shape(CTX, PAIRS + 1, 2, N), 4 * 10**7, 10**6, "fresh", LARGE
    )(x_input, b_input, step, log_decay)
    send, swap = lax.optimization_barrier((send, swap))
    flat = swap.reshape(NX, 2, 8, NTP, COLS).transpose(2, 0, 1, 3, 4).reshape(8, NX * 2 * NTP * COLS)
    weight = lax.all_gather(flat, "z", axis=0).reshape(NZ, 8, NX, 2, NTP, COLS)
    weight = weight.transpose(0, 2, 3, 1, 4, 5).reshape(NZ, NX, depth, NTP * COLS)

    got = lax.all_to_all(send, ("x", "z"), 0, 0, tiled=True)
    inner, scale = call(
        inner_kernel,
        (shape(TOK, WIDTH, dtype=f32), shape(TOK, WIDTH, dtype=f32)),
        10**8,
        2 * 10**6,
        "inner",
    )(x_input, b_input, c_input, step, log_decay, jnp.repeat(skip, P_SIZE)[None])
    entering = call(scan_kernel, shape(CTX, CHUNK, N), 10**6, 7 * 10**5, "scan")(got)
    states = lax.all_to_all(entering, ("x", "z"), 0, 0, tiled=True)

    hidden = call(hidden_kernel, shape(NX, TOK, WIDTH), 3 * 10**7, 2 * 10**6, "hidden")(
        inner, scale, c_input, states, gain[None]
    )
    everyone = lax.all_to_all(hidden, "x", 0, 0, tiled=True)
    other = product(everyone, weight, 1)
    other = lax.ppermute(other, "c", [(0, 1), (1, 0)])
    mine = product(everyone, weight, 0)
    parts = call(pair_kernel, shape(NX, NY, TOK, COLS), 10**6, 2 * 10**6, "pair")(mine, other)
    parts = lax.all_to_all(parts.reshape(NX * NY, TOK, COLS), ("x", "y"), 0, 0, tiled=True)
    return call(sum_kernel, shape(TOK, NX * COLS), 10**6, 10**6, "sum")(
        parts.reshape(NX, NY, TOK, COLS)
    )


def solution(mesh):
    fine = Mesh(mesh.devices.reshape(NX, NZ, NY, NC), ("x", "z", "y", "c"))
    ctx, tp = ("x", "z"), ("y", "c")
    in_specs = (
        P(ctx, tp),
        P(ctx, tp),
        P(ctx, tp),
        P(tp, ctx),
        P(tp, ctx),
        P(tp),
        P(tp),
        P(tp + ctx, None),
    )
    return jax.shard_map(
        shards, mesh=fine, in_specs=in_specs, out_specs=P(ctx, tp), check_vma=False
    )
```
